32 devices in a mesh: groups: 2 (over x), samp: 8 (over z, y), line: 2 (over core).
Axes of the slice: x: 2, y: 2, z: 4, core: 2. Of those that a mesh axis runs over, the one named last changes fastest.
Arguments:
- cube: float32 [7077888], P(('groups', 'samp', 'line')), parts along dimension 0, may hold values from -4000 to 4000
Outputs:
- details1: float32 [5308416], P(('groups', 'samp', 'line')), parts along dimension 0
- details2: float32 [1327104], P(('groups', 'samp', 'line')), parts along dimension 0
- details3: float32 [331776], P(('groups', 'samp', 'line')), parts along dimension 0
- approx: float32 [110592], P(('groups', 'samp', 'line')), parts along dimension 0
The draws below stay inside these ranges and needn't reach their ends.
There are 2 independent parts, one for each index of `groups`. The reference program is written for one: setup_inputs(seed, part) draws one part's arguments, and reference() takes and returns one part's arrays. A program takes and returns all parts, laid end to end along the dimension named above; each array names one. Nothing has to cross between parts.
All inputs are finite; a program needn't handle non-finite values.
Results may differ from the reference program's by a relative error of at most 0.000088.
Values sent between devices are 32-bit elements; how exact they have to be, the bound alone decides.
No kernel may reach another device: no remote copies, remote signals or barrier semaphores. Data moves between devices by JAX's collectives and lax.ppermute only.
A program may use at most 64 MiB of HBM per device.

```python
import math
import jax
import jax.numpy as jnp
from jax import lax

BANDS = 432
LD = 32
SD = 16
LINES = 64
SAMPLES = 128
NPIX = 8192
N_SAMP = 8
N_LINE = 2


def draw_cube(key, part):
    subkeys = jax.random.split(key, 4)
    log_ten = math.log(10.0)
    band_scale = jnp.exp(jax.random.uniform(subkeys[0], (BANDS, 1, 1), jnp.float32, 0.0, log_ten))
    offset = jax.random.uniform(subkeys[1], (BANDS, 1, 1), jnp.float32, -1.0, 1.0)
    sample_ramp = 1.0 + 2.0 * jnp.arange(SAMPLES, dtype=jnp.float32) / (SAMPLES - 1)
    pixel_scale = jnp.exp(jax.random.uniform(subkeys[2], (1, LINES, SAMPLES), jnp.float32, 0.0, log_ten)) * sample_ramp
    fresh_noise = jnp.clip(jax.random.normal(subkeys[3], (BANDS, LINES, SAMPLES), jnp.float32), -4.0, 4.0)
    common = jnp.zeros((1, LINES, SAMPLES), jnp.float32)
    blended = fresh_noise + 0.6 * jnp.roll(fresh_noise, 1, 0) + 0.4 * jnp.roll(fresh_noise, 2, 0)
    image = band_scale * (offset + common + pixel_scale * blended)
    shaped = image.reshape(BANDS, LINES // LD, LD, SAMPLES // SD, SD)
    return jnp.transpose(shaped, (3, 1, 0, 2, 4)).reshape(-1)


def setup_inputs(seed: int = 0, part: int = 0) -> dict:
    splits = jax.random.split(jax.random.key(seed), 2)
    part_splits = jax.random.split(jax.random.fold_in(splits[1], part), 2)
    return {
        "cube": draw_cube(jax.random.fold_in(jax.random.fold_in(splits[1], part), 71), part),
    }


alpha_lift = -1.586134342059924
beta_lift = -0.052980118572961
gamma_lift = 0.882911075530934
delta_lift = 0.443506852043971
scale_lift = 1.230174104914001

def split_pairs(values, axis):
    length = values.shape[axis]
    return (lax.slice_in_dim(values, 0, length, 2, axis), lax.slice_in_dim(values, 1, length, 2, axis))

def lift(values, axis):
    evens, odds = split_pairs(values, axis)
    half = evens.shape[axis]
    for weight_odd, weight_even in ((alpha_lift, beta_lift), (gamma_lift, delta_lift)):
        following = jnp.concatenate([lax.slice_in_dim(evens, 1, half, 1, axis), lax.slice_in_dim(evens, half - 1, half, 1, axis)], axis)
        odds = odds + weight_odd * (evens + following)
        preceding = jnp.concatenate([lax.slice_in_dim(odds, 0, 1, 1, axis), lax.slice_in_dim(odds, 0, half - 1, 1, axis)], axis)
        evens = evens + weight_even * (preceding + odds)
    return (evens / scale_lift, odds * scale_lift)

def subbands(values):
    low_s, high_s = lift(values, 2)
    low_l, high_l = lift(jnp.concatenate([low_s, high_s], 2), 1)
    middle = low_s.shape[2]
    details = jnp.stack([high_l[:, :, :middle], low_l[:, :, middle:], high_l[:, :, middle:]])
    return (low_l[:, :, :middle], details)

def to_tiles(values, level):
    tile_lines = LD // level
    tile_samples = SD // level
    lead = values.shape[:-2]
    count = len(lead)
    shaped = values.reshape(lead + (N_LINE, tile_lines, N_SAMP, tile_samples))
    order = (count + 2, count) + tuple(range(count)) + (count + 1, count + 3)
    return jnp.transpose(shaped, order).reshape(-1)

def reference(cube):
    tiled = cube.reshape(N_SAMP, N_LINE, BANDS, LD, SD)
    image = jnp.transpose(tiled, (2, 1, 3, 0, 4)).reshape(BANDS, LD * N_LINE, SD * N_SAMP)
    band_count = BANDS
    flattened = image.reshape(band_count, -1)
    band_mean = jnp.sum(flattened, axis=1) / NPIX
    centered = flattened - band_mean[:, None]
    covariance = jnp.dot(centered.astype(jnp.float32), centered.T.astype(jnp.float32), precision=lax.Precision.HIGHEST, preferred_element_type=jnp.float32) / NPIX
    identity = jnp.eye(band_count, dtype=covariance.dtype)
    regular = covariance + 0.01 * (jnp.trace(covariance) / band_count) * identity
    factor = jnp.linalg.cholesky(regular)
    whitener = lax.linalg.triangular_solve(factor, identity, left_side=True, lower=True)
    components = jnp.dot(whitener.astype(jnp.float32), centered.astype(jnp.float32), precision=lax.Precision.HIGHEST, preferred_element_type=jnp.float32).reshape(image.shape)
    approx1, level1 = subbands(components)
    approx2, level2 = subbands(approx1)
    approx3, level3 = subbands(approx2)
    return (to_tiles(level1, 2), to_tiles(level2, 4), to_tiles(level3, 8), to_tiles(approx3, 8))
```

```python
import functools

import numpy as np
import jax
import jax.numpy as jnp
from jax import lax
from jax.experimental import pallas as pl
from jax.experimental.pallas import tpu as pltpu
from jax.sharding import PartitionSpec as P

BANDS = 432
LD = 32
SD = 16
LANES = 128
BLOCK = 128

alpha_lift = -1.586134342059924
beta_lift = -0.052980118572961
gamma_lift = 0.882911075530934
delta_lift = 0.443506852043971
scale_lift = 1.230174104914001

HIGHEST = lax.Precision.HIGHEST


def product(left, right, left_dim, right_dim):
    return lax.dot_general(
        left,
        right,
        (((left_dim,), (right_dim,)), ((), ())),
        precision=HIGHEST,
        preferred_element_type=jnp.float32,
    )


def lift_rows(values):
    evens, odds = values[0::2], values[1::2]
    for weight_odd, weight_even in ((alpha_lift, beta_lift), (gamma_lift, delta_lift)):
        following = np.concatenate([evens[1:], evens[-1:]])
        odds = odds + weight_odd * (evens + following)
        preceding = np.concatenate([odds[:1], odds[:-1]])
        evens = evens + weight_even * (preceding + odds)
    return evens / scale_lift, odds * scale_lift


def axis_operators(length):
    operators = {}
    current = np.eye(length)
    for level in (1, 2, 3):
        low, high = lift_rows(current)
        operators[level, 0], operators[level, 1] = low, high
        current = low
    return operators


def output_lanes():
    lanes = []
    for level in (1, 2, 3):
        parts = [(1, 0), (0, 1), (1, 1)] + ([(0, 0)] if level == 3 else [])
        for line_part, samp_part in parts:
            for line in range(LD >> level):
                for samp in range(SD >> level):
                    lanes.append((level, line_part, samp_part, line, samp))
    return lanes


def factor_tables(n_samp, n_line):
    lanes = output_lanes()
    line_ops = axis_operators(LD * n_line)
    samp_ops = axis_operators(SD * n_samp)
    count = len(lanes)
    line_table = np.zeros((n_line, n_line * LD, count))
    for q in range(n_line):
        order = [q] + [other for other in range(n_line) if other != q]
        for o, (level, part, _, line, _) in enumerate(lanes):
            row = line_ops[level, part][q * (LD >> level) + line]
            for k, source in enumerate(order):
                line_table[q, k * LD : (k + 1) * LD, o] = row[source * LD : (source + 1) * LD]
    reach = {}
    for step in (0, -1, 1, -2, 2):
        table = np.zeros((n_samp, SD, count))
        for p in range(n_samp):
            target = p + step
            if 0 <= target < n_samp:
                for o, (level, _, part, _, samp) in enumerate(lanes):
                    row = samp_ops[level, part][target * (SD >> level) + samp]
                    table[p, :, o] = row[p * SD : (p + 1) * SD]
        reach[step] = table
    return line_table, reach


SENDS = ((-1, 256), (1, 256), (-2, 128), (2, 128))


def build_constants(n_samp, n_line):
    line_table, reach = factor_tables(n_samp, n_line)
    count = line_table.shape[2]
    line_parts, samp_parts = [line_table], [reach[0]]
    selections, offsets = [], []
    line_sums = line_table.sum(1)
    for step, width in SENDS:
        used = np.nonzero(np.abs(reach[step]).sum((0, 1)))[0]
        assert len(used) < width
        line_cols = np.zeros((n_line, n_line * LD, width))
        samp_cols = np.zeros((n_samp, SD, width))
        line_cols[:, :, : len(used)] = line_table[:, :, used]
        samp_cols[:, :, : len(used)] = reach[step][:, :, used]
        line_parts.append(line_cols)
        samp_parts.append(samp_cols)
        chosen = np.full((width, 1), -1, np.int32)
        chosen[: len(used), 0] = used
        selections.append(np.broadcast_to(chosen, (width, LANES)))
        sums = np.zeros((n_samp, count))
        for p in range(n_samp):
            if 0 <= p - step < n_samp:
                sums[p] = reach[step][p - step].sum(0)
        offsets.append(sums)
    whole = np.zeros((n_samp, count))
    for p in range(n_samp):
        for step in reach:
            if 0 <= p - step < n_samp:
                whole[p] += reach[step][p - step].sum(0)
    offsets.append(whole)
    offset_table = np.zeros((n_samp, n_line, 8, count))
    for k, sums in enumerate(offsets):
        offset_table[:, :, k] = sums[:, None] * line_sums[None]
    return (
        np.concatenate(line_parts, 2).astype(np.float32),
        np.concatenate(samp_parts, 2).astype(np.float32),
        np.concatenate(selections, 0).astype(np.int32),
        offset_table.astype(np.float32),
    )


EDGES = list(range(0, BANDS, BLOCK)) + [BANDS]
LAST = EDGES[-1] - EDGES[-2]
OFF_DIAGONAL = ((1, 0), (2, 0), (2, 1), (3, 0), (3, 1), (3, 2))


def payload_rows(tiles):
    places = {}
    row = 2 * BLOCK
    for i, j in OFF_DIAGONAL:
        places[i, j] = row
        row += EDGES[i + 1] - EDGES[i]
    places["diagonal"] = row
    row += 8
    places["means"] = row
    row += 4 * tiles
    return places, -(-row // 32) * 32


def square_iotas():
    rows = lax.broadcasted_iota(jnp.int32, (BLOCK, BLOCK), 0)
    cols = lax.broadcasted_iota(jnp.int32, (BLOCK, BLOCK), 1)
    return rows, cols


def gram_kernel(tiles, where_ref, x_ref, send_ref, keep_ref, mean_ref, xs, pack):
    places, total = payload_rows(tiles)
    half = total // 2
    tile, line = where_ref[0], where_ref[1]
    per_row = LD * SD // LANES
    parts = [x_ref[pl.ds(c, BANDS, stride=per_row), :] for c in range(per_row)]
    mean = jnp.sum(sum(parts[1:], parts[0]), axis=1, keepdims=True) / (LD * SD)
    mean_ref[...] = jnp.broadcast_to(mean, (BANDS, LANES))
    for c in range(per_row):
        xs[0:BANDS, c * LANES : (c + 1) * LANES] = parts[c] - mean
    xs[BANDS:, :] = jnp.zeros_like(xs[BANDS:, :])
    rows, cols = square_iotas()

    def block(i, j):
        return product(
            xs[i * BLOCK : (i + 1) * BLOCK, :], xs[j * BLOCK : (j + 1) * BLOCK, :], 1, 1
        )

    pack[places["diagonal"] :, :] = jnp.zeros_like(pack[places["diagonal"] :, :])
    for k in range(2):
        lower, upper = block(2 * k, 2 * k), block(2 * k + 1, 2 * k + 1)
        pack[k * BLOCK : (k + 1) * BLOCK, :] = jnp.where(rows >= cols, lower, upper)
        pack[places["diagonal"] + k : places["diagonal"] + k + 1, :] = jnp.sum(
            jnp.where(rows == cols, upper, 0.0), axis=0, keepdims=True
        )
    for i, j in OFF_DIAGONAL:
        height = EDGES[i + 1] - EDGES[i]
        pack[places[i, j] : places[i, j] + height, :] = block(i, j)[:height]
    lane = lax.broadcasted_iota(jnp.int32, (BANDS, LANES), 1)
    mean_row = product(
        jnp.ones((8, LANES), jnp.float32), jnp.where(lane == 0, mean, 0.0), 1, 1
    )
    which = lax.broadcasted_iota(jnp.int32, (tiles, BLOCK), 0)
    for c in range(4):
        width = EDGES[c + 1] - EDGES[c]
        place = places["means"] + c * tiles
        pack[place : place + tiles, 0:width] = jnp.where(
            which[:, :width] == tile, mean_row[0:1, EDGES[c] : EDGES[c + 1]], 0.0
        )
    keep_ref[...] = pack[pl.ds(pl.multiple_of(line * half, 8), half), :]
    send_ref[...] = pack[pl.ds(pl.multiple_of((1 - line) * half, 8), half), :]


def wavelet_kernel(x_ref, other_ref, mean_ref, line_ref, samp_ref, *rest):
    own_ref, sends, (xs, matrix) = rest[0], rest[1:5], rest[5:]
    per_row = LD * SD // LANES
    mean = mean_ref[...]
    for k, ref in enumerate((x_ref, other_ref)):
        for c in range(per_row):
            at = (k * per_row + c) * LANES
            xs[:, at : at + LANES] = ref[pl.ds(c, BANDS, stride=per_row), :] - mean

    def columns(start, width):
        samp = samp_ref[:, start : start + width]
        for line in range(2 * LD):
            matrix[line * SD : (line + 1) * SD, 0:width] = (
                samp * line_ref[line : line + 1, start : start + width]
            )
        return product(xs[...], matrix[:, 0:width], 1, 0)

    for start in (0, 256):
        own_ref[:, start : start + 256] = columns(start, 256)
    start = own_ref.shape[1]
    for ref in sends:
        width = ref.shape[1]
        lane = lax.broadcasted_iota(jnp.int32, (BANDS, width), 1)
        wide = jnp.broadcast_to(mean[:, 0:1], (BANDS, width))
        ref[...] = jnp.where(lane == width - 1, wide, columns(start, width))
        start += width


def reciprocal(value):
    guess = pl.reciprocal(value, approx=True)
    return guess * (2.0 - value * guess)


def spread(value):
    return jnp.broadcast_to(value, (8, LANES))


def inverse_factor(groups):
    rows = list(groups)
    lane = lax.broadcasted_iota(jnp.int32, (8, LANES), 1)
    sub = lax.broadcasted_iota(jnp.int32, (8, LANES), 0)
    done = []
    for b in range(len(rows)):
        base = 8 * b
        current = rows[b]
        cols = [spread(current[:, base + t : base + t + 1]) for t in range(8)]
        s = [[spread(cols[t][u : u + 1, :]) if u >= t else None for t in range(8)] for u in range(8)]
        inside = (lane >= base) & (lane < base + 8)
        start = jnp.where(inside, jnp.where(lane == base + sub, 1.0, 0.0), current)
        y = [spread(start[t : t + 1, :]) for t in range(8)]
        r = [None] * 8
        l = [[None] * 8 for _ in range(8)]
        for p in range(8):
            r[p] = reciprocal(s[p][p])
            for t in range(p + 1, 8):
                l[t][p] = s[t][p] * r[p]
            for t in range(p + 1, 8):
                for u in range(t, 8):
                    s[u][t] = s[u][t] - s[u][p] * l[t][p]
                y[t] = y[t] - l[t][p] * y[p]
        z = [None] * 8
        for t in range(7, -1, -1):
            z[t] = r[t] * y[t]
            for u in range(t + 1, 8):
                z[t] = z[t] - l[u][t] * z[u]
        for g in range(b + 1, len(rows)):
            old = rows[g]
            terms = [spread(old[:, base + t : base + t + 1]) * z[t] for t in range(8)]
            while len(terms) > 1:
                terms = [terms[k] + terms[k + 1] for k in range(0, len(terms), 2)]
            rows[g] = jnp.where(inside, 0.0, old) - terms[0]
        q, d = y[0], s[0][0]
        for t in range(1, 8):
            q = jnp.where(sub == t, y[t], q)
            d = jnp.where(sub == t, s[t][t], d)
        done.append(jnp.where(lane < base + 8, q * lax.rsqrt(d), 0.0))
    return done


def whiten_kernel(tiles, where_ref, mine_ref, theirs_ref, w_ref, dev_ref, pack, a):
    places, total = payload_rows(tiles)
    half = total // 2
    line = where_ref[1]
    pack[pl.ds(pl.multiple_of(line * half, 8), half), :] = mine_ref[...]
    pack[pl.ds(pl.multiple_of((1 - line) * half, 8), half), :] = theirs_ref[...]
    at = places["means"]
    means = jnp.concatenate([pack[at + c * tiles : at + (c + 1) * tiles, :] for c in range(4)], 1)
    dev = means - jnp.sum(means, axis=0, keepdims=True) / tiles
    dev_ref[...] = dev
    between = (LD * SD) * product(dev, dev, 0, 0)
    rows, cols = square_iotas()
    trace = jnp.zeros((1, BLOCK), jnp.float32)
    for k in range(2):
        packed = pack[k * BLOCK : (k + 1) * BLOCK, :]
        turned = packed.T
        diagonal = pack[places["diagonal"] + k : places["diagonal"] + k + 1, :]
        lower = jnp.where(rows >= cols, packed, turned)
        upper = jnp.where(rows < cols, packed, jnp.where(rows > cols, turned, diagonal))
        for i, full in ((2 * k, lower), (2 * k + 1, upper)):
            low, high = EDGES[i], EDGES[i + 1]
            full = full + between[i * BLOCK : (i + 1) * BLOCK, i * BLOCK : (i + 1) * BLOCK]
            trace += jnp.sum(jnp.where(rows == cols, full, 0.0), axis=0, keepdims=True)
            a[low:high, i * BLOCK : (i + 1) * BLOCK] = full[: high - low]
    for i, j in OFF_DIAGONAL:
        low, high = EDGES[i], EDGES[i + 1]
        a[low:high, j * BLOCK : (j + 1) * BLOCK] = (
            pack[places[i, j] : places[i, j] + high - low, :]
            + between[low:high, j * BLOCK : (j + 1) * BLOCK]
        )
    load = 0.01 * (jnp.sum(trace, axis=1, keepdims=True) / BANDS)
    for i in range(4):
        low, high = EDGES[i], EDGES[i + 1]
        full = a[low:high, i * BLOCK : (i + 1) * BLOCK]
        height = high - low
        a[low:high, i * BLOCK : (i + 1) * BLOCK] = full + jnp.where(
            (rows == cols)[:height], load, 0.0
        )
    w_ref[...] = jnp.zeros_like(w_ref)
    for k in range(4):
        low, high = EDGES[k], EDGES[k + 1]
        groups = [a[low + 8 * g : low + 8 * g + 8, low : low + BLOCK] for g in range((high - low) // 8)]
        m = jnp.concatenate(inverse_factor(groups), 0)[:, : high - low]
        if k:
            w_ref[low:high, :low] = product(m, w_ref[low:high, :low], 1, 0)
        w_ref[low:high, low:high] = m
        if high < BANDS:
            factor = product(a[high:, low:high], m, 1, 1)
            for j in range(k + 1, 4):
                below = factor[EDGES[j] - high :]
                a[EDGES[j] :, EDGES[j] : EDGES[j + 1]] -= product(
                    below, below[: EDGES[j + 1] - EDGES[j]], 1, 1
                )
            w_ref[high:, :high] = w_ref[high:, :high] - product(factor, w_ref[low:high, :high], 1, 0)


def output_kernel(pixels, where_ref, own_ref, mean_ref, dev_ref, w_ref, offset_ref, chosen_ref, *rest):
    arrived, (out1_ref, out2_ref, out3_ref, approx_ref), (d, small) = rest[:4], rest[4:8], rest[8:]
    tile = where_ref[0]
    count = own_ref.shape[1]
    mean = mean_ref[...]
    tiles = dev_ref.shape[0]
    which = lax.broadcasted_iota(jnp.int32, (tiles, count), 0)
    total = own_ref[...] + product(
        dev_ref[:, 0:BANDS], jnp.where(which == tile, offset_ref[4:5, :], 0.0), 0, 0
    )
    start = 0
    for k, ref in enumerate(arrived):
        width = ref.shape[1]
        lane = lax.broadcasted_iota(jnp.int32, (BANDS, width), 1)
        wide = jnp.broadcast_to(mean[:, 0:1], (BANDS, width))
        values = ref[...] - jnp.where(lane == width - 1, wide, 0.0)
        chosen = jnp.broadcast_to(chosen_ref[start : start + width, 0:1], (width, count))
        columns = lax.broadcasted_iota(jnp.int32, (width, count), 1)
        row = lax.broadcasted_iota(jnp.int32, (width, count), 0)
        select = jnp.where(row == width - 1, offset_ref[k : k + 1, :], jnp.where(chosen == columns, 1.0, 0.0))
        total += product(values, select, 1, 0)
        start += width
    d[...] = total * (float(pixels) ** 0.5)
    for k in range(4):
        low, high = EDGES[k], EDGES[k + 1]
        out = product(w_ref[low:high, :high], d[0:high, :], 1, 0)
        for sb in range(3):
            out1_ref[sb * BANDS + low : sb * BANDS + high, :] = out[:, sb * LANES : (sb + 1) * LANES]
        small[low:high, :] = out[:, 3 * LANES :]

    def repack(first, width):
        together = LANES // width
        height = BANDS // together
        lane = lax.broadcasted_iota(jnp.int32, (height, LANES), 1)
        result = jnp.zeros((height, LANES), jnp.float32)
        for k in range(together):
            taken = small[pl.ds(k, height, stride=together), :]
            moved = pltpu.roll(taken, (k * width - first) % LANES, 1)
            result = jnp.where((lane >= k * width) & (lane < (k + 1) * width), moved, result)
        return result

    size2, size3 = (LD // 4) * (SD // 4), (LD // 8) * (SD // 8)
    rows2, rows3 = BANDS * size2 // LANES, BANDS * size3 // LANES
    for sb in range(3):
        out2_ref[sb * rows2 : (sb + 1) * rows2, :] = repack(sb * size2, size2)
        out3_ref[sb * rows3 : (sb + 1) * rows3, :] = repack(3 * size2 + sb * size3, size3)
    approx_ref[...] = repack(3 * size2 + 3 * size3, size3)


def swapped(array, axis, bit):
    return lax.ppermute(array, axis, [(i, i ^ bit) for i in range(lax.axis_size(axis))])


def shifted(array, axis, step):
    count = lax.axis_size(axis)
    return lax.ppermute(array, axis, [(i, i + step) for i in range(count) if 0 <= i + step < count])


VMEM = pl.BlockSpec(memory_space=pltpu.VMEM)
SMEM = pl.BlockSpec(memory_space=pltpu.SMEM)


def call(kernel, shapes, inputs, scratch, flops):
    specs = [SMEM if value.dtype == jnp.int32 and value.ndim == 1 else VMEM for value in inputs]
    size = sum(value.size * 4 for value in inputs)
    return pl.pallas_call(
        kernel,
        out_shape=[jax.ShapeDtypeStruct(shape, jnp.float32) for shape in shapes],
        in_specs=specs,
        out_specs=[VMEM] * len(shapes),
        scratch_shapes=[pltpu.VMEM(shape, jnp.float32) for shape in scratch],
        compiler_params=pltpu.CompilerParams(vmem_limit_bytes=40 * 2**20),
        cost_estimate=pl.CostEstimate(flops=flops, bytes_accessed=size, transcendentals=0),
    )(*inputs)


def local(constants, cube):
    line_table, samp_table, chosen, offset_table = constants
    n_samp, n_line = lax.axis_size("samp"), lax.axis_size("line")
    tiles = n_samp * n_line
    samp, line = lax.axis_index("samp"), lax.axis_index("line")
    where = jnp.stack([samp * n_line + line, line]).astype(jnp.int32)
    count = LD * SD
    x = cube.reshape(BANDS * count // LANES, LANES)
    other = swapped(x, "line", 1)
    _, total = payload_rows(tiles)
    half = total // 2
    send, keep, mean = call(
        functools.partial(gram_kernel, tiles),
        [(half, LANES), (half, LANES), (BANDS, LANES)],
        [where, x],
        [(4 * BLOCK, count), (total, LANES)],
        2 * BANDS * BANDS * count * 4,
    )
    summed = keep + swapped(send, "line", 1)
    bit = samp & 1
    quarter = half // 2
    kept = lax.dynamic_slice_in_dim(summed, bit * quarter, quarter, 0)
    given = lax.dynamic_slice_in_dim(summed, (1 - bit) * quarter, quarter, 0)
    kept = kept + swapped(given, "samp", 1)
    step = 2
    while step < n_samp:
        kept = kept + swapped(kept, "samp", step)
        step *= 2
    back = swapped(kept, "samp", 1)
    mine = jnp.where(bit == 0, jnp.concatenate([kept, back]), jnp.concatenate([back, kept]))
    theirs = swapped(mine, "line", 1)

    own, *sends = call(
        wavelet_kernel,
        [(BANDS, count)] + [(BANDS, width) for _, width in SENDS],
        [x, other, mean, jnp.asarray(line_table)[line], jnp.asarray(samp_table)[samp]],
        [(BANDS, 2 * count), (2 * count, 256)],
        2 * BANDS * 2 * count * line_table.shape[2] * 6,
    )
    arrived = [shifted(value, "samp", step) for value, (step, _) in zip(sends, SENDS)]

    w, dev = call(
        functools.partial(whiten_kernel, tiles),
        [(BANDS, BANDS), (tiles, 4 * BLOCK)],
        [where, mine, theirs],
        [(total, LANES), (BANDS, 4 * BLOCK)],
        2 * 10**10,
    )
    outs = call(
        functools.partial(output_kernel, count * tiles),
        [
            (3 * BANDS * (count // 4) // LANES, LANES),
            (3 * BANDS * (count // 16) // LANES, LANES),
            (3 * BANDS * (count // 64) // LANES, LANES),
            (BANDS * (count // 64) // LANES, LANES),
        ],
        [where, own, mean, dev, w, jnp.asarray(offset_table)[samp, line], jnp.asarray(chosen)] + arrived,
        [(BANDS, count), (BANDS, LANES)],
        2 * BANDS * BANDS * count * 6,
    )
    return tuple(out.reshape(-1) for out in outs)


def solution(mesh):
    n_samp, n_line = mesh.shape["samp"], mesh.shape["line"]
    assert n_line == 2 and n_samp & (n_samp - 1) == 0
    constants = build_constants(n_samp, n_line)
    spec = P(("groups", "samp", "line"))
    return jax.shard_map(
        functools.partial(local, constants),
        mesh=mesh,
        in_specs=(spec,),
        out_specs=(spec,) * 4,
        check_vma=False,
    )
```

```python
import functools

import numpy as np
import jax
import jax.numpy as jnp
from jax import lax
from jax.experimental import pallas as pl
from jax.experimental.pallas import tpu as pltpu
from jax.sharding import PartitionSpec as P

BANDS = 432
LD = 32
SD = 16
LANES = 128
BLOCK = 128

alpha_lift = -1.586134342059924
beta_lift = -0.052980118572961
gamma_lift = 0.882911075530934
delta_lift = 0.443506852043971
scale_lift = 1.230174104914001

HIGHEST = lax.Precision.HIGHEST


def product(left, right, left_dim, right_dim):
    return lax.dot_general(
        left,
        right,
        (((left_dim,), (right_dim,)), ((), ())),
        precision=HIGHEST,
        preferred_element_type=jnp.float32,
    )


def lift_rows(values):
    evens, odds = values[0::2], values[1::2]
    for weight_odd, weight_even in ((alpha_lift, beta_lift), (gamma_lift, delta_lift)):
        following = np.concatenate([evens[1:], evens[-1:]])
        odds = odds + weight_odd * (evens + following)
        preceding = np.concatenate([odds[:1], odds[:-1]])
        evens = evens + weight_even * (preceding + odds)
    return evens / scale_lift, odds * scale_lift


def axis_operators(length):
    operators = {}
    current = np.eye(length)
    for level in (1, 2, 3):
        low, high = lift_rows(current)
        operators[level, 0], operators[level, 1] = low, high
        current = low
    return operators


def output_lanes():
    lanes = []
    for level in (1, 2, 3):
        parts = [(1, 0), (0, 1), (1, 1)] + ([(0, 0)] if level == 3 else [])
        for line_part, samp_part in parts:
            for line in range(LD >> level):
                for samp in range(SD >> level):
                    lanes.append((level, line_part, samp_part, line, samp))
    return lanes


def factor_tables(n_samp, n_line):
    lanes = output_lanes()
    line_ops = axis_operators(LD * n_line)
    samp_ops = axis_operators(SD * n_samp)
    count = len(lanes)
    line_table = np.zeros((n_line, n_line * LD, count))
    for q in range(n_line):
        order = [q] + [other for other in range(n_line) if other != q]
        for o, (level, part, _, line, _) in enumerate(lanes):
            row = line_ops[level, part][q * (LD >> level) + line]
            for k, source in enumerate(order):
                line_table[q, k * LD : (k + 1) * LD, o] = row[source * LD : (source + 1) * LD]
    reach = {}
    for step in (0, -1, 1, -2, 2):
        table = np.zeros((n_samp, SD, count))
        for p in range(n_samp):
            target = p + step
            if 0 <= target < n_samp:
                for o, (level, _, part, _, samp) in enumerate(lanes):
                    row = samp_ops[level, part][target * (SD >> level) + samp]
                    table[p, :, o] = row[p * SD : (p + 1) * SD]
        reach[step] = table
    return line_table, reach


SENDS = ((-1, 256), (1, 256), (-2, 128), (2, 128))


def build_constants(n_samp, n_line):
    line_table, reach = factor_tables(n_samp, n_line)
    count = line_table.shape[2]
    line_parts, samp_parts = [line_table], [reach[0]]
    selections, offsets = [], []
    line_sums = line_table.sum(1)
    for step, width in SENDS:
        used = np.nonzero(np.abs(reach[step]).sum((0, 1)))[0]
        assert len(used) < width
        line_cols = np.zeros((n_line, n_line * LD, width))
        samp_cols = np.zeros((n_samp, SD, width))
        line_cols[:, :, : len(used)] = line_table[:, :, used]
        samp_cols[:, :, : len(used)] = reach[step][:, :, used]
        line_parts.append(line_cols)
        samp_parts.append(samp_cols)
        chosen = np.full((width, 1), -1, np.int32)
        chosen[: len(used), 0] = used
        selections.append(np.broadcast_to(chosen, (width, LANES)))
        sums = np.zeros((n_samp, count))
        for p in range(n_samp):
            if 0 <= p - step < n_samp:
                sums[p] = reach[step][p - step].sum(0)
        offsets.append(sums)
    whole = np.zeros((n_samp, count))
    for p in range(n_samp):
        for step in reach:
            if 0 <= p - step < n_samp:
                whole[p] += reach[step][p - step].sum(0)
    offsets.append(whole)
    offset_table = np.zeros((n_samp, n_line, 8, count))
    for k, sums in enumerate(offsets):
        offset_table[:, :, k] = sums[:, None] * line_sums[None]
    return (
        np.concatenate(line_parts, 2).astype(np.float32),
        np.concatenate(samp_parts, 2).astype(np.float32),
        np.concatenate(selections, 0).astype(np.int32),
        offset_table.astype(np.float32),
    )


EDGES = list(range(0, BANDS, BLOCK)) + [BANDS]
LAST = EDGES[-1] - EDGES[-2]
OFF_DIAGONAL = ((1, 0), (2, 0), (2, 1), (3, 0), (3, 1), (3, 2))


def payload_rows(tiles):
    places = {}
    row = 2 * BLOCK
    for i, j in OFF_DIAGONAL:
        places[i, j] = row
        row += EDGES[i + 1] - EDGES[i]
    places["diagonal"] = row
    row += 8
    places["means"] = row
    row += 4 * tiles
    return places, -(-row // 32) * 32


def square_iotas():
    rows = lax.broadcasted_iota(jnp.int32, (BLOCK, BLOCK), 0)
    cols = lax.broadcasted_iota(jnp.int32, (BLOCK, BLOCK), 1)
    return rows, cols


def gram_kernel(tiles, where_ref, x_ref, send_ref, keep_ref, mean_ref, xs, pack):
    places, total = payload_rows(tiles)
    half = total // 2
    tile, line = where_ref[0], where_ref[1]
    per_row = LD * SD // LANES
    parts = [x_ref[pl.ds(c, BANDS, stride=per_row), :] for c in range(per_row)]
    mean = jnp.sum(sum(parts[1:], parts[0]), axis=1, keepdims=True) / (LD * SD)
    mean_ref[...] = jnp.broadcast_to(mean, (BANDS, LANES))
    for c in range(per_row):
        xs[0:BANDS, c * LANES : (c + 1) * LANES] = parts[c] - mean
    xs[BANDS:, :] = jnp.zeros_like(xs[BANDS:, :])
    rows, cols = square_iotas()

    def block(i, j):
        return product(
            xs[i * BLOCK : (i + 1) * BLOCK, :], xs[j * BLOCK : (j + 1) * BLOCK, :], 1, 1
        )

    pack[places["diagonal"] :, :] = jnp.zeros_like(pack[places["diagonal"] :, :])
    for k in range(2):
        lower, upper = block(2 * k, 2 * k), block(2 * k + 1, 2 * k + 1)
        pack[k * BLOCK : (k + 1) * BLOCK, :] = jnp.where(rows >= cols, lower, upper)
        pack[places["diagonal"] + k : places["diagonal"] + k + 1, :] = jnp.sum(
            jnp.where(rows == cols, upper, 0.0), axis=0, keepdims=True
        )
    for i, j in OFF_DIAGONAL:
        height = EDGES[i + 1] - EDGES[i]
        pack[places[i, j] : places[i, j] + height, :] = block(i, j)[:height]
    lane = lax.broadcasted_iota(jnp.int32, (BANDS, LANES), 1)
    mean_row = product(
        jnp.ones((8, LANES), jnp.float32), jnp.where(lane == 0, mean, 0.0), 1, 1
    )
    which = lax.broadcasted_iota(jnp.int32, (tiles, BLOCK), 0)
    for c in range(4):
        width = EDGES[c + 1] - EDGES[c]
        place = places["means"] + c * tiles
        pack[place : place + tiles, 0:width] = jnp.where(
            which[:, :width] == tile, mean_row[0:1, EDGES[c] : EDGES[c + 1]], 0.0
        )
    keep_ref[...] = pack[pl.ds(pl.multiple_of(line * half, 8), half), :]
    send_ref[...] = pack[pl.ds(pl.multiple_of((1 - line) * half, 8), half), :]


def wavelet_kernel(x_ref, other_ref, mean_ref, line_ref, samp_ref, *rest):
    own_ref, sends, (xs, matrix) = rest[0], rest[1:5], rest[5:]
    per_row = LD * SD // LANES
    mean = mean_ref[...]
    for k, ref in enumerate((x_ref, other_ref)):
        for c in range(per_row):
            at = (k * per_row + c) * LANES
            xs[:, at : at + LANES] = ref[pl.ds(c, BANDS, stride=per_row), :] - mean

    def columns(start, width):
        samp = samp_ref[:, start : start + width]
        for line in range(2 * LD):
            matrix[line * SD : (line + 1) * SD, 0:width] = (
                samp * line_ref[line : line + 1, start : start + width]
            )
        return product(xs[...], matrix[:, 0:width], 1, 0)

    for start in (0, 256):
        own_ref[:, start : start + 256] = columns(start, 256)
    start = own_ref.shape[1]
    for ref in sends:
        width = ref.shape[1]
        lane = lax.broadcasted_iota(jnp.int32, (BANDS, width), 1)
        wide = jnp.broadcast_to(mean[:, 0:1], (BANDS, width))
        ref[...] = jnp.where(lane == width - 1, wide, columns(start, width))
        start += width


def spread(value):
    return jnp.broadcast_to(value, (8, LANES))


def added(terms):
    terms = list(terms)
    while len(terms) > 1:
        terms = [sum(terms[k + 1 : k + 2], terms[k]) for k in range(0, len(terms), 2)]
    return terms[0]


NEAR = 2


def inverse_factor(groups, held):
    rows = list(groups)
    lane = lax.broadcasted_iota(jnp.int32, (8, LANES), 1)
    sub = lax.broadcasted_iota(jnp.int32, (8, LANES), 0)
    done = []

    def columns(group, base):
        return [spread(group[:, base + t : base + t + 1]) for t in range(8)]

    following = columns(rows[0], 0)
    for b in range(len(rows)):
        base, slot = 8 * b, b % 2
        current = rows[b]
        for t in range(8):
            held[slot, t] = following[t]
        s = [[spread(held[slot, t, u : u + 1, :]) if u >= t else None for t in range(8)] for u in range(8)]
        inside = (lane >= base) & (lane < base + 8)
        start = jnp.where(inside, jnp.where(lane == base + sub, 1.0, 0.0), current)
        y = [spread(start[t : t + 1, :]) for t in range(8)]
        near = list(range(b + 1, min(len(rows), b + 1 + NEAR)))
        far = list(range(b + 1 + NEAR, len(rows)))
        g = {i: columns(rows[i], base) for i in near}
        if near:
            raw = columns(rows[b + 1], base + 8)
        r = [None] * 8
        l = [[None] * 8 for _ in range(8)]
        for p in range(8):
            r[p] = pl.reciprocal(s[p][p], approx=True)
            for t in range(p + 1, 8):
                l[t][p] = s[t][p] * r[p]
            for t in range(p + 1, 8):
                for u in range(t, 8):
                    if u == t == p + 1:
                        s[u][t] = s[u][t] - (s[u][p] * s[t][p]) * r[p]
                    else:
                        s[u][t] = s[u][t] - s[u][p] * l[t][p]
                for i in near:
                    g[i][t] = g[i][t] - g[i][p] * l[t][p]
                y[t] = y[t] - l[t][p] * y[p]
        scaled = {i: [g[i][p] * r[p] for p in range(8)] for i in near}
        if near:
            for p in range(8):
                held[slot, 8 + p] = scaled[b + 1][p]
            following = [
                raw[t] - added(g[b + 1][p] * spread(held[slot, 8 + p, t : t + 1, :]) for p in range(8))
                for t in range(8)
            ]
        for i in near:
            rows[i] = jnp.where(inside, 0.0, rows[i]) - added(scaled[i][p] * y[p] for p in range(8))
        if far:
            z = [None] * 8
            for t in range(7, -1, -1):
                z[t] = r[t] * y[t]
                for u in range(t + 1, 8):
                    z[t] = z[t] - l[u][t] * z[u]
            for i in far:
                old = columns(rows[i], base)
                rows[i] = jnp.where(inside, 0.0, rows[i]) - added(old[t] * z[t] for t in range(8))
        q, d = y[0], s[0][0]
        for t in range(1, 8):
            q = jnp.where(sub == t, y[t], q)
            d = jnp.where(sub == t, s[t][t], d)
        done.append(jnp.where(lane < base + 8, q * lax.rsqrt(d), 0.0))
    return done


def whiten_kernel(tiles, where_ref, mine_ref, theirs_ref, w_ref, dev_ref, pack, a, held):
    places, total = payload_rows(tiles)
    half = total // 2
    line = where_ref[1]
    pack[pl.ds(pl.multiple_of(line * half, 8), half), :] = mine_ref[...]
    pack[pl.ds(pl.multiple_of((1 - line) * half, 8), half), :] = theirs_ref[...]
    at = places["means"]
    means = jnp.concatenate([pack[at + c * tiles : at + (c + 1) * tiles, :] for c in range(4)], 1)
    dev = means - jnp.sum(means, axis=0, keepdims=True) / tiles
    dev_ref[...] = dev
    between = (LD * SD) * product(dev, dev, 0, 0)
    rows, cols = square_iotas()
    trace = jnp.zeros((1, BLOCK), jnp.float32)
    for k in range(2):
        packed = pack[k * BLOCK : (k + 1) * BLOCK, :]
        turned = packed.T
        diagonal = pack[places["diagonal"] + k : places["diagonal"] + k + 1, :]
        lower = jnp.where(rows >= cols, packed, turned)
        upper = jnp.where(rows < cols, packed, jnp.where(rows > cols, turned, diagonal))
        for i, full in ((2 * k, lower), (2 * k + 1, upper)):
            low, high = EDGES[i], EDGES[i + 1]
            full = full + between[i * BLOCK : (i + 1) * BLOCK, i * BLOCK : (i + 1) * BLOCK]
            trace += jnp.sum(jnp.where(rows == cols, full, 0.0), axis=0, keepdims=True)
            a[low:high, i * BLOCK : (i + 1) * BLOCK] = full[: high - low]
    for i, j in OFF_DIAGONAL:
        low, high = EDGES[i], EDGES[i + 1]
        a[low:high, j * BLOCK : (j + 1) * BLOCK] = (
            pack[places[i, j] : places[i, j] + high - low, :]
            + between[low:high, j * BLOCK : (j + 1) * BLOCK]
        )
    load = 0.01 * (jnp.sum(trace, axis=1, keepdims=True) / BANDS)
    for i in range(4):
        low, high = EDGES[i], EDGES[i + 1]
        full = a[low:high, i * BLOCK : (i + 1) * BLOCK]
        height = high - low
        a[low:high, i * BLOCK : (i + 1) * BLOCK] = full + jnp.where(
            (rows == cols)[:height], load, 0.0
        )
    w_ref[...] = jnp.zeros_like(w_ref)
    for k in range(4):
        low, high = EDGES[k], EDGES[k + 1]
        groups = [a[low + 8 * g : low + 8 * g + 8, low : low + BLOCK] for g in range((high - low) // 8)]
        m = jnp.concatenate(inverse_factor(groups, held), 0)[:, : high - low]
        if k:
            w_ref[low:high, :low] = product(m, w_ref[low:high, :low], 1, 0)
        w_ref[low:high, low:high] = m
        if high < BANDS:
            factor = product(a[high:, low:high], m, 1, 1)
            for j in range(k + 1, 4):
                below = factor[EDGES[j] - high :]
                a[EDGES[j] :, EDGES[j] : EDGES[j + 1]] -= product(
                    below, below[: EDGES[j + 1] - EDGES[j]], 1, 1
                )
            w_ref[high:, :high] = w_ref[high:, :high] - product(factor, w_ref[low:high, :high], 1, 0)


def output_kernel(pixels, where_ref, own_ref, mean_ref, dev_ref, w_ref, offset_ref, chosen_ref, *rest):
    arrived, (out1_ref, out2_ref, out3_ref, approx_ref), (d, small) = rest[:4], rest[4:8], rest[8:]
    tile = where_ref[0]
    count = own_ref.shape[1]
    mean = mean_ref[...]
    tiles = dev_ref.shape[0]
    which = lax.broadcasted_iota(jnp.int32, (tiles, count), 0)
    total = own_ref[...] + product(
        dev_ref[:, 0:BANDS], jnp.where(which == tile, offset_ref[4:5, :], 0.0), 0, 0
    )
    start = 0
    for k, ref in enumerate(arrived):
        width = ref.shape[1]
        lane = lax.broadcasted_iota(jnp.int32, (BANDS, width), 1)
        wide = jnp.broadcast_to(mean[:, 0:1], (BANDS, width))
        values = ref[...] - jnp.where(lane == width - 1, wide, 0.0)
        chosen = jnp.broadcast_to(chosen_ref[start : start + width, 0:1], (width, count))
        columns = lax.broadcasted_iota(jnp.int32, (width, count), 1)
        row = lax.broadcasted_iota(jnp.int32, (width, count), 0)
        select = jnp.where(row == width - 1, offset_ref[k : k + 1, :], jnp.where(chosen == columns, 1.0, 0.0))
        total += product(values, select, 1, 0)
        start += width
    d[...] = total * (float(pixels) ** 0.5)
    for k in range(4):
        low, high = EDGES[k], EDGES[k + 1]
        out = product(w_ref[low:high, :high], d[0:high, :], 1, 0)
        for sb in range(3):
            out1_ref[sb * BANDS + low : sb * BANDS + high, :] = out[:, sb * LANES : (sb + 1) * LANES]
        small[low:high, :] = out[:, 3 * LANES :]

    def repack(first, width):
        together = LANES // width
        height = BANDS // together
        lane = lax.broadcasted_iota(jnp.int32, (height, LANES), 1)
        result = jnp.zeros((height, LANES), jnp.float32)
        for k in range(together):
            taken = small[pl.ds(k, height, stride=together), :]
            moved = pltpu.roll(taken, (k * width - first) % LANES, 1)
            result = jnp.where((lane >= k * width) & (lane < (k + 1) * width), moved, result)
        return result

    size2, size3 = (LD // 4) * (SD // 4), (LD // 8) * (SD // 8)
    rows2, rows3 = BANDS * size2 // LANES, BANDS * size3 // LANES
    for sb in range(3):
        out2_ref[sb * rows2 : (sb + 1) * rows2, :] = repack(sb * size2, size2)
        out3_ref[sb * rows3 : (sb + 1) * rows3, :] = repack(3 * size2 + sb * size3, size3)
    approx_ref[...] = repack(3 * size2 + 3 * size3, size3)


def swapped(array, axis, bit):
    return lax.ppermute(array, axis, [(i, i ^ bit) for i in range(lax.axis_size(axis))])


def shifted(array, axis, step):
    count = lax.axis_size(axis)
    return lax.ppermute(array, axis, [(i, i + step) for i in range(count) if 0 <= i + step < count])


VMEM = pl.BlockSpec(memory_space=pltpu.VMEM)
SMEM = pl.BlockSpec(memory_space=pltpu.SMEM)


def call(kernel, shapes, inputs, scratch, flops):
    specs = [SMEM if value.dtype == jnp.int32 and value.ndim == 1 else VMEM for value in inputs]
    size = sum(value.size * 4 for value in inputs)
    return pl.pallas_call(
        kernel,
        out_shape=[jax.ShapeDtypeStruct(shape, jnp.float32) for shape in shapes],
        in_specs=specs,
        out_specs=[VMEM] * len(shapes),
        scratch_shapes=[pltpu.VMEM(shape, jnp.float32) for shape in scratch],
        compiler_params=pltpu.CompilerParams(vmem_limit_bytes=40 * 2**20),
        cost_estimate=pl.CostEstimate(flops=flops, bytes_accessed=size, transcendentals=0),
    )(*inputs)


def local(constants, cube):
    line_table, samp_table, chosen, offset_table = constants
    n_samp, n_line = lax.axis_size("samp"), lax.axis_size("line")
    tiles = n_samp * n_line
    samp, line = lax.axis_index("samp"), lax.axis_index("line")
    where = jnp.stack([samp * n_line + line, line]).astype(jnp.int32)
    count = LD * SD
    x = cube.reshape(BANDS * count // LANES, LANES)
    other = swapped(x, "line", 1)
    _, total = payload_rows(tiles)
    half = total // 2
    send, keep, mean = call(
        functools.partial(gram_kernel, tiles),
        [(half, LANES), (half, LANES), (BANDS, LANES)],
        [where, x],
        [(4 * BLOCK, count), (total, LANES)],
        2 * BANDS * BANDS * count * 4,
    )
    summed = keep + swapped(send, "line", 1)
    bit = samp & 1
    quarter = half // 2
    kept = lax.dynamic_slice_in_dim(summed, bit * quarter, quarter, 0)
    given = lax.dynamic_slice_in_dim(summed, (1 - bit) * quarter, quarter, 0)
    kept = kept + swapped(given, "samp", 1)
    step = 2
    while step < n_samp:
        kept = kept + swapped(kept, "samp", step)
        step *= 2
    back = swapped(kept, "samp", 1)
    mine = jnp.where(bit == 0, jnp.concatenate([kept, back]), jnp.concatenate([back, kept]))
    theirs = swapped(mine, "line", 1)

    own, *sends = call(
        wavelet_kernel,
        [(BANDS, count)] + [(BANDS, width) for _, width in SENDS],
        [x, other, mean, jnp.asarray(line_table)[line], jnp.asarray(samp_table)[samp]],
        [(BANDS, 2 * count), (2 * count, 256)],
        2 * BANDS * 2 * count * line_table.shape[2] * 6,
    )
    arrived = [shifted(value, "samp", step) for value, (step, _) in zip(sends, SENDS)]

    w, dev = call(
        functools.partial(whiten_kernel, tiles),
        [(BANDS, BANDS), (tiles, 4 * BLOCK)],
        [where, mine, theirs],
        [(total, LANES), (BANDS, 4 * BLOCK), (2, 16, 8, LANES)],
        2 * 10**10,
    )
    outs = call(
        functools.partial(output_kernel, count * tiles),
        [
            (3 * BANDS * (count // 4) // LANES, LANES),
            (3 * BANDS * (count // 16) // LANES, LANES),
            (3 * BANDS * (count // 64) // LANES, LANES),
            (BANDS * (count // 64) // LANES, LANES),
        ],
        [where, own, mean, dev, w, jnp.asarray(offset_table)[samp, line], jnp.asarray(chosen)] + arrived,
        [(BANDS, count), (BANDS, LANES)],
        2 * BANDS * BANDS * count * 6,
    )
    return tuple(out.reshape(-1) for out in outs)


def solution(mesh):
    n_samp, n_line = mesh.shape["samp"], mesh.shape["line"]
    assert n_line == 2 and n_samp & (n_samp - 1) == 0
    constants = build_constants(n_samp, n_line)
    spec = P(("groups", "samp", "line"))
    return jax.shard_map(
        functools.partial(local, constants),
        mesh=mesh,
        in_specs=(spec,),
        out_specs=(spec,) * 4,
        check_vma=False,
    )
```

```python
import functools

import numpy as np
import jax
import jax.numpy as jnp
from jax import lax
from jax.experimental import pallas as pl
from jax.experimental.pallas import tpu as pltpu
from jax.sharding import PartitionSpec as P

BANDS = 432
LD = 32
SD = 16
LANES = 128
BLOCK = 128

alpha_lift = -1.586134342059924
beta_lift = -0.052980118572961
gamma_lift = 0.882911075530934
delta_lift = 0.443506852043971
scale_lift = 1.230174104914001


def split3(value):
    high = value.astype(jnp.bfloat16)
    rest = value - high.astype(jnp.float32)
    middle = rest.astype(jnp.bfloat16)
    return high, middle, (rest - middle.astype(jnp.float32)).astype(jnp.bfloat16)


def left_terms(parts, dim):
    high, middle, low = parts
    return jnp.concatenate([high, high, middle, high, low, middle], dim)


def right_terms(parts, dim):
    high, middle, low = parts
    return jnp.concatenate([high, middle, high, low, high, middle], dim)


def product_parts(left, right, left_dim, right_dim):
    return lax.dot_general(
        left_terms(left, left_dim),
        right_terms(right, right_dim),
        (((left_dim,), (right_dim,)), ((), ())),
        preferred_element_type=jnp.float32,
    )


def product(left, right, left_dim, right_dim):
    return product_parts(split3(left), split3(right), left_dim, right_dim)


def lift_rows(values):
    evens, odds = values[0::2], values[1::2]
    for weight_odd, weight_even in ((alpha_lift, beta_lift), (gamma_lift, delta_lift)):
        following = np.concatenate([evens[1:], evens[-1:]])
        odds = odds + weight_odd * (evens + following)
        preceding = np.concatenate([odds[:1], odds[:-1]])
        evens = evens + weight_even * (preceding + odds)
    return evens / scale_lift, odds * scale_lift


def axis_operators(length):
    operators = {}
    current = np.eye(length)
    for level in (1, 2, 3):
        low, high = lift_rows(current)
        operators[level, 0], operators[level, 1] = low, high
        current = low
    return operators


def output_lanes():
    lanes = []
    for level in (1, 2, 3):
        parts = [(1, 0), (0, 1), (1, 1)] + ([(0, 0)] if level == 3 else [])
        for line_part, samp_part in parts:
            for line in range(LD >> level):
                for samp in range(SD >> level):
                    lanes.append((level, line_part, samp_part, line, samp))
    return lanes


GROUP = LANES // SD
TILE_GROUPS = LD // GROUP
SHALLOW = (TILE_GROUPS + 1) * LANES
WIDE = SD // 2
LEVEL1 = 3 * (LD // 2) * WIDE
COUNT = LD * SD
FAR = COUNT // 16


def strip_lines(q):
    own = list(range(q * LD, (q + 1) * LD))
    groups = [list(range((1 - q) * LD + g * GROUP, (1 - q) * LD + (g + 1) * GROUP)) for g in range(TILE_GROUPS)]
    if q == 1:
        groups = groups[::-1]
    return own + [line for group in groups for line in group]


def neighbour_steps(p):
    near, far = 1 - 2 * (p & 1), 2 - 2 * (p & 2)
    return near, -near, far, -far


def build_constants(n_samp, n_line):
    lanes = output_lanes()
    line_ops = axis_operators(LD * n_line)
    samp_ops = axis_operators(SD * n_samp)
    line_own = np.zeros((n_line, n_line * LD, COUNT))
    for q in range(n_line):
        order = strip_lines(q)
        for o, (level, part, _, line, _) in enumerate(lanes):
            line_own[q, :, o] = line_ops[level, part][q * (LD >> level) + line][order]
    assert not line_own[:, SHALLOW // SD :, :LEVEL1].any()

    def reach(p, step):
        table = np.zeros((SD, COUNT))
        if 0 <= p + step < n_samp:
            for o, (level, _, part, _, samp) in enumerate(lanes):
                row = samp_ops[level, part][(p + step) * (SD >> level) + samp]
                table[:, o] = row[p * SD : (p + 1) * SD]
        return table

    size = COUNT + 5 * LANES
    line_table = np.zeros((n_line, n_line * LD, size))
    samp_table = np.zeros((n_samp, SD, size))
    line_table[:, :, :COUNT] = line_own
    for k in range(2):
        at = COUNT + k * LANES
        for line in range(LD // 2):
            for sb in range(3):
                for j in range(2):
                    source = (sb * (LD // 2) + line) * WIDE
                    line_table[:, :, at + line * WIDE + 2 * sb + j] = line_own[:, :, source]
        at = COUNT + (2 + k) * LANES
        line_table[:, :, at : at + LANES] = line_own[:, :, LEVEL1:]
        at = COUNT + 4 * LANES + k * FAR
        line_table[:, :, at : at + FAR] = line_own[:, :, COUNT - FAR :]
    offsets = np.zeros((n_samp, n_line, 8, COUNT))
    line_sums = line_own.sum(1)
    for p in range(n_samp):
        samp_table[p, :, :COUNT] = reach(p, 0)
        whole = reach(p, 0).sum(0)
        for k, step in enumerate(neighbour_steps(p)):
            given = reach(p, step)
            if k < 2:
                base = 0 if step > 0 else WIDE - 2
                left = given.copy()
                for line in range(LD // 2):
                    for sb in range(3):
                        for j in range(2):
                            source = (sb * (LD // 2) + line) * WIDE + base + j
                            samp_table[p, :, COUNT + k * LANES + line * WIDE + 2 * sb + j] = given[:, source]
                            left[:, source] = 0.0
                assert not left[:, :LEVEL1].any()
                at = COUNT + (2 + k) * LANES
                samp_table[p, :, at : at + LANES] = given[:, LEVEL1:]
            else:
                assert not given[:, : COUNT - FAR].any()
                at = COUNT + 4 * LANES + (k - 2) * FAR
                samp_table[p, :, at : at + FAR] = given[:, COUNT - FAR :]
            if 0 <= p + step < n_samp:
                sums = reach(p + step, -step).sum(0)
                offsets[p, :, k] = sums * line_sums
                whole = whole + sums
        offsets[p, :, 4] = whole * line_sums
        offsets[p, :, 4] -= offsets[p, :, :4].sum(1)
    return line_table.astype(np.float32), samp_table.astype(np.float32), offsets.astype(np.float32)


EDGES = list(range(0, BANDS, BLOCK)) + [BANDS]
LAST = EDGES[-1] - EDGES[-2]
OFF_DIAGONAL = ((1, 0), (2, 0), (2, 1), (3, 0), (3, 1), (3, 2))


def payload_rows(tiles):
    places = {}
    row = 2 * BLOCK
    for i, j in OFF_DIAGONAL:
        places[i, j] = row
        row += EDGES[i + 1] - EDGES[i]
    places["diagonal"] = row
    row += 8
    places["means"] = row
    row += 4 * tiles
    return places, -(-row // 32) * 32


def square_iotas():
    rows = lax.broadcasted_iota(jnp.int32, (BLOCK, BLOCK), 0)
    cols = lax.broadcasted_iota(jnp.int32, (BLOCK, BLOCK), 1)
    return rows, cols


def gram_kernel(tiles, where_ref, x_ref, send_ref, keep_ref, mean_ref, xs, pack):
    places, total = payload_rows(tiles)
    half = total // 2
    tile, line = where_ref[0], where_ref[1]
    parts = [x_ref[pl.ds(c, BANDS, stride=TILE_GROUPS), :] for c in range(TILE_GROUPS)]
    mean = jnp.sum(sum(parts[1:], parts[0]), axis=1, keepdims=True) / COUNT
    mean_ref[...] = jnp.broadcast_to(mean, (BANDS, LANES))
    for c in range(TILE_GROUPS):
        for k, part in enumerate(split3(parts[c] - mean)):
            xs[k, 0:BANDS, c * LANES : (c + 1) * LANES] = part
    xs[:, BANDS:, :] = jnp.zeros_like(xs[:, BANDS:, :])
    rows, cols = square_iotas()

    def rows_of(i):
        return [xs[k, 2 * i * BLOCK : 2 * (i + 1) * BLOCK, :] for k in range(3)]

    blocks = {}
    for i, j in ((0, 0), (1, 0), (1, 1)):
        square = product_parts(rows_of(i), rows_of(j), 1, 1)
        for a in range(2):
            for b in range(2):
                blocks[2 * i + a, 2 * j + b] = square[
                    a * BLOCK : (a + 1) * BLOCK, b * BLOCK : (b + 1) * BLOCK
                ]
    pack[places["diagonal"] :, :] = jnp.zeros_like(pack[places["diagonal"] :, :])
    for k in range(2):
        lower, upper = blocks[2 * k, 2 * k], blocks[2 * k + 1, 2 * k + 1]
        pack[k * BLOCK : (k + 1) * BLOCK, :] = jnp.where(rows >= cols, lower, upper)
        pack[places["diagonal"] + k : places["diagonal"] + k + 1, :] = jnp.sum(
            jnp.where(rows == cols, upper, 0.0), axis=0, keepdims=True
        )
    for i, j in OFF_DIAGONAL:
        height = EDGES[i + 1] - EDGES[i]
        pack[places[i, j] : places[i, j] + height, :] = blocks[i, j][:height]
    lane = lax.broadcasted_iota(jnp.int32, (BANDS, LANES), 1)
    mean_row = sum(
        lax.dot_general(
            jnp.ones((16, LANES), jnp.bfloat16),
            part,
            (((1,), (1,)), ((), ())),
            preferred_element_type=jnp.float32,
        )
        for part in split3(jnp.where(lane == 0, mean, 0.0))
    )
    which = lax.broadcasted_iota(jnp.int32, (tiles, BLOCK), 0)
    for c in range(4):
        width = EDGES[c + 1] - EDGES[c]
        place = places["means"] + c * tiles
        pack[place : place + tiles, 0:width] = jnp.where(
            which[:, :width] == tile, mean_row[0:1, EDGES[c] : EDGES[c + 1]], 0.0
        )
    keep_ref[...] = pack[pl.ds(pl.multiple_of(line * half, 8), half), :]
    send_ref[...] = pack[pl.ds(pl.multiple_of((1 - line) * half, 8), half), :]


def load_strip(where_ref, x_ref, other_ref, mean_ref, xs):
    mean = mean_ref[...]
    line = where_ref[1]
    for g in range(2 * TILE_GROUPS):
        if g < TILE_GROUPS:
            block = x_ref[pl.ds(g, BANDS, stride=TILE_GROUPS), :]
        else:
            k = g - TILE_GROUPS
            at = k + line * (TILE_GROUPS - 1 - 2 * k)
            block = other_ref[pl.ds(at, BANDS, stride=TILE_GROUPS), :]
        for k, part in enumerate(split3(block - mean)):
            xs[k, :, g * LANES : (g + 1) * LANES] = part


def strip_product(line_ref, samp_ref, xs, matrix, start, width, depth):
    samp = samp_ref[:, start : start + width]
    for line in range(depth // SD):
        values = samp * line_ref[line : line + 1, start : start + width]
        for k, part in enumerate(split3(values)):
            matrix[k, line * SD : (line + 1) * SD, 0:width] = part
    return product_parts(
        [xs[k, :, 0:depth] for k in range(3)], [matrix[k, 0:depth, 0:width] for k in range(3)], 1, 0
    )


def repacked(small, first, width):
    together = LANES // width
    height = BANDS // together
    lane = lax.broadcasted_iota(jnp.int32, (height, LANES), 1)
    result = jnp.zeros((height, LANES), jnp.float32)
    for k in range(together):
        taken = small[pl.ds(k, height, stride=together), :]
        moved = pltpu.roll(taken, (k * width - first) % LANES, 1)
        result = jnp.where((lane >= k * width) & (lane < (k + 1) * width), moved, result)
    return result


FAR_ROWS = BANDS * FAR // LANES
FAR_HELD = -(-FAR_ROWS // 8) * 8


def contribution_kernel(
    where_ref, x_ref, other_ref, mean_ref, line_ref, samp_ref, near1, near2, far1, far2, xs, matrix, small
):
    load_strip(where_ref, x_ref, other_ref, mean_ref, xs)
    run = functools.partial(strip_product, line_ref, samp_ref, xs, matrix)
    small[...] = run(COUNT + 4 * LANES, LANES, 2 * COUNT)
    for k, ref in enumerate((far1, far2)):
        ref[FAR_ROWS:, :] = jnp.zeros_like(ref[FAR_ROWS:, :])
        ref[0:FAR_ROWS, :] = repacked(small, k * FAR, FAR)
    first = run(COUNT, 2 * LANES, SHALLOW)
    near1[:, 0:LANES] = first[:, 0:LANES]
    near2[:, 0:LANES] = first[:, LANES:]
    second = run(COUNT + 2 * LANES, 2 * LANES, 2 * COUNT)
    near1[:, LANES:] = second[:, 0:LANES]
    near2[:, LANES:] = second[:, LANES:]


def own_kernel(where_ref, x_ref, other_ref, mean_ref, line_ref, samp_ref, own_ref, xs, matrix):
    load_strip(where_ref, x_ref, other_ref, mean_ref, xs)
    run = functools.partial(strip_product, line_ref, samp_ref, xs, matrix)
    own_ref[:, 0:LEVEL1] = run(0, LEVEL1, SHALLOW)
    own_ref[:, LEVEL1:] = run(LEVEL1, COUNT - LEVEL1, 2 * COUNT)


def spread(value):
    return jnp.broadcast_to(value, (8, LANES))


def added(terms):
    terms = list(terms)
    while len(terms) > 1:
        terms = [sum(terms[k + 1 : k + 2], terms[k]) for k in range(0, len(terms), 2)]
    return terms[0]


NEAR = 2


def inverse_factor(groups, held):
    rows = list(groups)
    lane = lax.broadcasted_iota(jnp.int32, (8, LANES), 1)
    sub = lax.broadcasted_iota(jnp.int32, (8, LANES), 0)
    done = []

    def columns(group, base):
        return [spread(group[:, base + t : base + t + 1]) for t in range(8)]

    following = columns(rows[0], 0)
    for b in range(len(rows)):
        base, slot = 8 * b, b % 2
        current = rows[b]
        for t in range(8):
            held[slot, t] = following[t]
        s = [[spread(held[slot, t, u : u + 1, :]) if u >= t else None for t in range(8)] for u in range(8)]
        inside = (lane >= base) & (lane < base + 8)
        start = jnp.where(inside, jnp.where(lane == base + sub, 1.0, 0.0), current)
        y = [spread(start[t : t + 1, :]) for t in range(8)]
        near = list(range(b + 1, min(len(rows), b + 1 + NEAR)))
        far = list(range(b + 1 + NEAR, len(rows)))
        g = {i: columns(rows[i], base) for i in near}
        if near:
            raw = columns(rows[b + 1], base + 8)
        r = [None] * 8
        l = [[None] * 8 for _ in range(8)]
        for p in range(8):
            r[p] = pl.reciprocal(s[p][p], approx=True)
            for t in range(p + 1, 8):
                l[t][p] = s[t][p] * r[p]
            for t in range(p + 1, 8):
                for u in range(t, 8):
                    if u == t == p + 1:
                        s[u][t] = s[u][t] - (s[u][p] * s[t][p]) * r[p]
                    else:
                        s[u][t] = s[u][t] - s[u][p] * l[t][p]
                for i in near:
                    g[i][t] = g[i][t] - g[i][p] * l[t][p]
                y[t] = y[t] - l[t][p] * y[p]
        scaled = {i: [g[i][p] * r[p] for p in range(8)] for i in near}
        if near:
            for p in range(8):
                held[slot, 8 + p] = scaled[b + 1][p]
            following = [
                raw[t] - added(g[b + 1][p] * spread(held[slot, 8 + p, t : t + 1, :]) for p in range(8))
                for t in range(8)
            ]
        for i in near:
            rows[i] = jnp.where(inside, 0.0, rows[i]) - added(scaled[i][p] * y[p] for p in range(8))
        if far:
            z = [None] * 8
            for t in range(7, -1, -1):
                z[t] = r[t] * y[t]
                for u in range(t + 1, 8):
                    z[t] = z[t] - l[u][t] * z[u]
            for i in far:
                old = columns(rows[i], base)
                rows[i] = jnp.where(inside, 0.0, rows[i]) - added(old[t] * z[t] for t in range(8))
        q, d = y[0], s[0][0]
        for t in range(1, 8):
            q = jnp.where(sub == t, y[t], q)
            d = jnp.where(sub == t, s[t][t], d)
        done.append(jnp.where(lane < base + 8, q * lax.rsqrt(d), 0.0))
    return done


def whiten_kernel(tiles, where_ref, mine_ref, theirs_ref, w_ref, dev_ref, pack, a, held):
    places, total = payload_rows(tiles)
    half = total // 2
    line = where_ref[1]
    pack[pl.ds(pl.multiple_of(line * half, 8), half), :] = mine_ref[...]
    pack[pl.ds(pl.multiple_of((1 - line) * half, 8), half), :] = theirs_ref[...]
    at = places["means"]
    means = jnp.concatenate([pack[at + c * tiles : at + (c + 1) * tiles, :] for c in range(4)], 1)
    dev = means - jnp.sum(means, axis=0, keepdims=True) / tiles
    dev_ref[...] = dev
    between = (LD * SD) * product(dev, dev, 0, 0)
    rows, cols = square_iotas()
    trace = jnp.zeros((1, BLOCK), jnp.float32)
    for k in range(2):
        packed = pack[k * BLOCK : (k + 1) * BLOCK, :]
        turned = packed.T
        diagonal = pack[places["diagonal"] + k : places["diagonal"] + k + 1, :]
        lower = jnp.where(rows >= cols, packed, turned)
        upper = jnp.where(rows < cols, packed, jnp.where(rows > cols, turned, diagonal))
        for i, full in ((2 * k, lower), (2 * k + 1, upper)):
            low, high = EDGES[i], EDGES[i + 1]
            full = full + between[i * BLOCK : (i + 1) * BLOCK, i * BLOCK : (i + 1) * BLOCK]
            trace += jnp.sum(jnp.where(rows == cols, full, 0.0), axis=0, keepdims=True)
            a[low:high, i * BLOCK : (i + 1) * BLOCK] = full[: high - low]
    for i, j in OFF_DIAGONAL:
        low, high = EDGES[i], EDGES[i + 1]
        a[low:high, j * BLOCK : (j + 1) * BLOCK] = (
            pack[places[i, j] : places[i, j] + high - low, :]
            + between[low:high, j * BLOCK : (j + 1) * BLOCK]
        )
    load = 0.01 * (jnp.sum(trace, axis=1, keepdims=True) / BANDS)
    for i in range(4):
        low, high = EDGES[i], EDGES[i + 1]
        full = a[low:high, i * BLOCK : (i + 1) * BLOCK]
        height = high - low
        a[low:high, i * BLOCK : (i + 1) * BLOCK] = full + jnp.where(
            (rows == cols)[:height], load, 0.0
        )
    w_ref[...] = jnp.zeros_like(w_ref)
    for k in range(4):
        low, high = EDGES[k], EDGES[k + 1]
        groups = [a[low + 8 * g : low + 8 * g + 8, low : low + BLOCK] for g in range((high - low) // 8)]
        m = jnp.concatenate(inverse_factor(groups, held), 0)[:, : high - low]
        if k:
            w_ref[low:high, :low] = product(m, w_ref[low:high, :low], 1, 0)
        w_ref[low:high, low:high] = m
        if high < BANDS:
            parts = split3(m)
            factor = split3(product_parts(split3(a[high:, low:high]), parts, 1, 1))
            a[high:, high:BANDS] = a[high:, high:BANDS] - product_parts(factor, factor, 1, 1)
            w_ref[high:, :high] = w_ref[high:, :high] - product_parts(factor, split3(w_ref[low:high, :high]), 1, 0)


def output_kernel(
    n_line, pixels, where_ref, own_ref, dev_ref, w_ref, offset_ref, near1, near2, far_ref, *rest
):
    (out1_ref, out2_ref, out3_ref, approx_ref), (d, small) = rest[:4], rest[4:]
    tile, samp = where_ref[0], where_ref[2]
    bit = samp % 2
    tiles = dev_ref.shape[0]
    which = lax.broadcasted_iota(jnp.int32, (tiles, COUNT), 0)
    near, far = 1 - 2 * bit, 2 - 4 * ((samp // 2) % 2)
    gains = jnp.where(which == tile, offset_ref[4:5, :], 0.0)
    for k, step in enumerate((near, -near, far, -far)):
        gains += jnp.where(which == tile + n_line * step, offset_ref[k : k + 1, :], 0.0)
    shift = product(dev_ref[:, 0:BANDS], gains, 0, 0)
    together = LANES // FAR
    lane = lax.broadcasted_iota(jnp.int32, (FAR_ROWS, LANES), 1)
    for k in range(together):
        moved = pltpu.roll(far_ref[0:FAR_ROWS, :], LANES - FAR - k * FAR, 1)
        small[pl.ds(k, FAR_ROWS, stride=together), :] = jnp.where(lane >= LANES - FAR, moved, 0.0)
    lane = lax.broadcasted_iota(jnp.int32, (BANDS, LANES), 1) % WIDE
    scale = float(pixels) ** 0.5

    def keep(at, value):
        for k, part in enumerate(split3(value * scale)):
            d[k, :, at : at + LANES] = part

    bases = ((WIDE - 2) * (1 - bit), (WIDE - 2) * bit)
    for sb in range(3):
        at = sb * LANES
        value = own_ref[:, at : at + LANES] + shift[:, at : at + LANES]
        for base, ref in zip(bases, (near1, near2)):
            moved = pltpu.roll(ref[:, 0:LANES], (base - 2 * sb + LANES) % LANES, 1)
            value += jnp.where((lane >= base) & (lane < base + 2), moved, 0.0)
        keep(at, value)
    keep(
        LEVEL1,
        own_ref[:, LEVEL1:] + shift[:, LEVEL1:] + near1[:, LANES:] + near2[:, LANES:] + small[...],
    )
    for low, high in ((0, 2 * BLOCK), (2 * BLOCK, BANDS)):
        w = split3(w_ref[low:high, :high])
        out = product_parts(w, [d[k, 0:high, :] for k in range(3)], 1, 0)
        for sb in range(3):
            out1_ref[sb * BANDS + low : sb * BANDS + high, :] = out[:, sb * LANES : (sb + 1) * LANES]
        small[low:high, :] = out[:, LEVEL1:]
    size2, size3 = COUNT // 16, COUNT // 64
    rows2, rows3 = BANDS * size2 // LANES, BANDS * size3 // LANES
    for sb in range(3):
        out2_ref[sb * rows2 : (sb + 1) * rows2, :] = repacked(small, sb * size2, size2)
        out3_ref[sb * rows3 : (sb + 1) * rows3, :] = repacked(small, 3 * size2 + sb * size3, size3)
    approx_ref[...] = repacked(small, 3 * size2 + 3 * size3, size3)


def permuted(array, axis, partner):
    count = lax.axis_size(axis)
    return lax.ppermute(array, axis, [(i, partner(i)) for i in range(count) if 0 <= partner(i) < count])


def mirrored(size):
    def partner(i):
        within = i % size
        return i - within + 2 * (size // 2 - 1 - within // 2) + within % 2

    return partner


VMEM = pl.BlockSpec(memory_space=pltpu.VMEM)
SMEM = pl.BlockSpec(memory_space=pltpu.SMEM)


def call(kernel, name, shapes, inputs, scratch, flops):
    specs = [SMEM if value.dtype == jnp.int32 and value.ndim == 1 else VMEM for value in inputs]
    size = sum(value.size * 4 for value in inputs)
    return pl.pallas_call(
        kernel,
        name=name,
        out_shape=[jax.ShapeDtypeStruct(shape, jnp.float32) for shape in shapes],
        in_specs=specs,
        out_specs=[VMEM] * len(shapes),
        scratch_shapes=[pltpu.VMEM(shape, dtype) for shape, dtype in scratch],
        compiler_params=pltpu.CompilerParams(vmem_limit_bytes=40 * 2**20),
        cost_estimate=pl.CostEstimate(flops=flops, bytes_accessed=size, transcendentals=0),
    )(*inputs)


def local(constants, cube):
    line_table, samp_table, offset_table = (jnp.asarray(table) for table in constants)
    n_samp, n_line = lax.axis_size("samp"), lax.axis_size("line")
    tiles = n_samp * n_line
    samp, line = lax.axis_index("samp"), lax.axis_index("line")
    where = jnp.stack([samp * n_line + line, line, samp]).astype(jnp.int32)
    f32, bf16 = jnp.float32, jnp.bfloat16
    x = cube.reshape(BANDS * COUNT // LANES, LANES)
    other = permuted(x, "line", lambda i: i ^ 1)
    _, total = payload_rows(tiles)
    half, quarter = total // 2, total // 4
    send, keep, mean = call(
        functools.partial(gram_kernel, tiles),
        "gram",
        [(half, LANES), (half, LANES), (BANDS, LANES)],
        [where, x],
        [((3, 4 * BLOCK, COUNT), bf16), ((total, LANES), f32)],
        2 * BANDS * BANDS * COUNT * 4,
    )
    summed = keep + permuted(send, "line", lambda i: i ^ 1)
    side = ((samp >> 1) ^ (samp >> 2)) & 1
    kept = lax.dynamic_slice_in_dim(summed, side * quarter, quarter, 0)
    given = lax.dynamic_slice_in_dim(summed, (1 - side) * quarter, quarter, 0)
    kept = kept + permuted(given, "samp", lambda i: i ^ 2)

    strip_scratch = [((3, BANDS, 2 * COUNT), bf16), ((3, 2 * COUNT, LEVEL1), bf16)]
    lines, samps = line_table[line], samp_table[samp]
    near1, near2, far1, far2 = call(
        contribution_kernel,
        "contributions",
        [(BANDS, 2 * LANES)] * 2 + [(FAR_HELD, LANES)] * 2,
        [where, x, other, mean, lines, samps],
        strip_scratch + [((BANDS, LANES), f32)],
        2 * BANDS * 2 * COUNT * 5 * LANES * 6,
    )
    kept, near1, near2 = lax.optimization_barrier((kept, near1, near2))
    kept2 = kept + permuted(kept, "samp", lambda i: i ^ 1)
    mean_later, _ = lax.optimization_barrier((mean, kept))
    (own,) = call(
        own_kernel,
        "own",
        [(BANDS, COUNT)],
        [where, x, other, mean_later, lines, samps],
        strip_scratch,
        2 * BANDS * 2 * COUNT * COUNT * 6,
    )
    kept, own = lax.optimization_barrier((kept2, own))
    far = jnp.zeros_like(far2)
    size = 8
    while size <= n_samp:
        partner = mirrored(size)
        both = permuted(jnp.concatenate([kept, far2]), "samp", partner)
        kept = kept + both[:quarter]
        adjacent = jnp.asarray([abs(partner(i) - i) == 2 for i in range(n_samp)])[samp]
        far = far + jnp.where(adjacent, both[quarter:], 0.0)
        size *= 2
    both = permuted(jnp.concatenate([kept, far1]), "samp", lambda i: i ^ 2)
    back = both[:quarter]
    far = far + both[quarter:]
    mine = jnp.where(side == 0, jnp.concatenate([kept, back]), jnp.concatenate([back, kept]))
    theirs = permuted(mine, "line", lambda i: i ^ 1)
    near1 = permuted(near1, "samp", lambda i: i ^ 1)
    near2 = permuted(near2, "samp", lambda i: ((i + 1) ^ 1) - 1)

    w, dev = call(
        functools.partial(whiten_kernel, tiles),
        "whiten",
        [(BANDS, BANDS), (tiles, 4 * BLOCK)],
        [where, mine, theirs],
        [((total, LANES), f32), ((BANDS, 4 * BLOCK), f32), ((2, 16, 8, LANES), f32)],
        2 * 10**10,
    )
    outs = call(
        functools.partial(output_kernel, n_line, COUNT * tiles),
        "outputs",
        [
            (3 * BANDS * (COUNT // 4) // LANES, LANES),
            (3 * BANDS * (COUNT // 16) // LANES, LANES),
            (3 * BANDS * (COUNT // 64) // LANES, LANES),
            (BANDS * (COUNT // 64) // LANES, LANES),
        ],
        [where, own, dev, w, offset_table[samp, line], near1, near2, far],
        [((3, BANDS, COUNT), bf16), ((BANDS, LANES), f32)],
        2 * BANDS * BANDS * COUNT * 6,
    )
    return tuple(out.reshape(-1) for out in outs)


def solution(mesh):
    n_samp, n_line = mesh.shape["samp"], mesh.shape["line"]
    assert n_line == 2 and n_samp >= 8 and n_samp & (n_samp - 1) == 0
    constants = build_constants(n_samp, n_line)
    spec = P(("groups", "samp", "line"))
    return jax.shard_map(
        functools.partial(local, constants),
        mesh=mesh,
        in_specs=(spec,),
        out_specs=(spec,) * 4,
        check_vma=False,
    )
```

```python
import functools

import numpy as np
import jax
import jax.numpy as jnp
from jax import lax
from jax.experimental import pallas as pl
from jax.experimental.pallas import tpu as pltpu
from jax.sharding import PartitionSpec as P

BANDS = 432
LD = 32
SD = 16
LANES = 128
BLOCK = 128

alpha_lift = -1.586134342059924
beta_lift = -0.052980118572961
gamma_lift = 0.882911075530934
delta_lift = 0.443506852043971
scale_lift = 1.230174104914001


def split3(value):
    high = value.astype(jnp.bfloat16)
    rest = value - high.astype(jnp.float32)
    middle = rest.astype(jnp.bfloat16)
    return high, middle, (rest - middle.astype(jnp.float32)).astype(jnp.bfloat16)


def left_terms(parts, dim):
    high, middle, low = parts
    return jnp.concatenate([high, high, middle, high, low, middle], dim)


def right_terms(parts, dim):
    high, middle, low = parts
    return jnp.concatenate([high, middle, high, low, high, middle], dim)


def product_parts(left, right, left_dim, right_dim):
    return lax.dot_general(
        left_terms(left, left_dim),
        right_terms(right, right_dim),
        (((left_dim,), (right_dim,)), ((), ())),
        preferred_element_type=jnp.float32,
    )


def product(left, right, left_dim, right_dim):
    return product_parts(split3(left), split3(right), left_dim, right_dim)


def lift_rows(values):
    evens, odds = values[0::2], values[1::2]
    for weight_odd, weight_even in ((alpha_lift, beta_lift), (gamma_lift, delta_lift)):
        following = np.concatenate([evens[1:], evens[-1:]])
        odds = odds + weight_odd * (evens + following)
        preceding = np.concatenate([odds[:1], odds[:-1]])
        evens = evens + weight_even * (preceding + odds)
    return evens / scale_lift, odds * scale_lift


def axis_operators(length):
    operators = {}
    current = np.eye(length)
    for level in (1, 2, 3):
        low, high = lift_rows(current)
        operators[level, 0], operators[level, 1] = low, high
        current = low
    return operators


def output_lanes():
    lanes = []
    for level in (1, 2, 3):
        parts = [(1, 0), (0, 1), (1, 1)] + ([(0, 0)] if level == 3 else [])
        for line_part, samp_part in parts:
            for line in range(LD >> level):
                for samp in range(SD >> level):
                    lanes.append((level, line_part, samp_part, line, samp))
    return lanes


GROUP = LANES // SD
TILE_GROUPS = LD // GROUP
SHALLOW = (TILE_GROUPS + 1) * LANES
WIDE = SD // 2
LEVEL1 = 3 * (LD // 2) * WIDE
COUNT = LD * SD
FAR = COUNT // 16


def strip_lines(q):
    own = list(range(q * LD, (q + 1) * LD))
    groups = [list(range((1 - q) * LD + g * GROUP, (1 - q) * LD + (g + 1) * GROUP)) for g in range(TILE_GROUPS)]
    if q == 1:
        groups = groups[::-1]
    return own + [line for group in groups for line in group]


def neighbour_steps(p):
    near = 1 - 2 * (p & 1)
    return near, -near, 2 * near, -2 * near


def relay_lanes(samp_ops, n_samp):
    lanes = output_lanes()
    pairs = []
    for parity in range(2):
        used = np.zeros((2, COUNT), bool)
        for p in range(n_samp):
            for k, step in enumerate((1 - 2 * parity, 2 - 4 * parity)):
                if 0 <= p + step < n_samp:
                    for o, (level, _, part, _, samp) in enumerate(lanes):
                        row = samp_ops[level, part][(p + step) * (SD >> level) + samp]
                        used[k, o] |= row[p * SD : (p + 1) * SD].any()
        free = [o - LEVEL1 for o in range(LEVEL1, COUNT) if not used[0, o]]
        wanted = [o for o in range(COUNT) if used[1, o]]
        assert len(wanted) <= len(free)
        pairs.append(list(zip(free, wanted)))
    return pairs


def build_constants(n_samp, n_line):
    lanes = output_lanes()
    line_ops = axis_operators(LD * n_line)
    samp_ops = axis_operators(SD * n_samp)
    line_own = np.zeros((n_line, n_line * LD, COUNT))
    for q in range(n_line):
        order = strip_lines(q)
        for o, (level, part, _, line, _) in enumerate(lanes):
            line_own[q, :, o] = line_ops[level, part][q * (LD >> level) + line][order]
    assert not line_own[:, SHALLOW // SD :, :LEVEL1].any()

    def reach(p, step):
        table = np.zeros((SD, COUNT))
        if 0 <= p + step < n_samp:
            for o, (level, _, part, _, samp) in enumerate(lanes):
                row = samp_ops[level, part][(p + step) * (SD >> level) + samp]
                table[:, o] = row[p * SD : (p + 1) * SD]
        return table

    size = COUNT + 5 * LANES
    relays = relay_lanes(samp_ops, n_samp)
    select = np.zeros((2, 2 * LANES, LANES))
    for parity in range(2):
        passed, moved = dict(relays[1 - parity]), dict(relays[parity])
        for lane in range(LANES):
            select[parity, lane, lane] = float(lane not in passed)
            select[parity, LANES + lane, moved[lane] - LEVEL1 if lane in moved else lane] = 1.0
    line_table = np.zeros((n_line, n_line * LD, size))
    samp_table = np.zeros((n_samp, SD, size))
    line_table[:, :, :COUNT] = line_own
    for k in range(2):
        at = COUNT + k * LANES
        for line in range(LD // 2):
            for sb in range(3):
                for j in range(2):
                    source = (sb * (LD // 2) + line) * WIDE
                    line_table[:, :, at + line * WIDE + 2 * sb + j] = line_own[:, :, source]
        at = COUNT + (2 + k) * LANES
        line_table[:, :, at : at + LANES] = line_own[:, :, LEVEL1:]
    at = COUNT + 4 * LANES
    line_table[:, :, at : at + FAR] = line_own[:, :, COUNT - FAR :]
    line_table = np.stack([line_table] * 2, 1)
    for parity in range(2):
        for lane, o in relays[parity]:
            line_table[:, parity, :, COUNT + 2 * LANES + lane] = line_own[:, :, o]
    offsets = np.zeros((n_samp, n_line, 8, COUNT))
    line_sums = line_own.sum(1)
    for p in range(n_samp):
        samp_table[p, :, :COUNT] = reach(p, 0)
        whole = reach(p, 0).sum(0)
        for k, step in enumerate(neighbour_steps(p)):
            given = reach(p, step)
            if k < 2:
                base = 0 if step > 0 else WIDE - 2
                left = given.copy()
                for line in range(LD // 2):
                    for sb in range(3):
                        for j in range(2):
                            source = (sb * (LD // 2) + line) * WIDE + base + j
                            samp_table[p, :, COUNT + k * LANES + line * WIDE + 2 * sb + j] = given[:, source]
                            left[:, source] = 0.0
                assert not left[:, :LEVEL1].any()
                at = COUNT + (2 + k) * LANES
                samp_table[p, :, at : at + LANES] = given[:, LEVEL1:]
            else:
                assert not given[:, : COUNT - FAR].any()
                if k == 2:
                    for lane, o in relays[p % 2]:
                        samp_table[p, :, COUNT + 2 * LANES + lane] = given[:, o]
                else:
                    at = COUNT + 4 * LANES
                    samp_table[p, :, at : at + FAR] = given[:, COUNT - FAR :]
            if 0 <= p + step < n_samp:
                sums = reach(p + step, -step).sum(0)
                offsets[p, :, k] = sums * line_sums
                whole = whole + sums
        offsets[p, :, 4] = whole * line_sums
        offsets[p, :, 4] -= offsets[p, :, :4].sum(1)
    relayed = np.zeros((2, 1, LANES), bool)
    for parity in range(2):
        relayed[parity, 0, [lane for lane, _ in relays[parity]]] = True
    return (
        line_table.astype(np.float32),
        samp_table.astype(np.float32),
        offsets.astype(np.float32),
        select.astype(np.float32),
        relayed,
    )


EDGES = list(range(0, BANDS, BLOCK)) + [BANDS]
LAST = EDGES[-1] - EDGES[-2]
OFF_DIAGONAL = ((1, 0), (2, 0), (2, 1), (3, 0), (3, 1), (3, 2))


def payload_rows(tiles):
    places = {}
    row = 2 * BLOCK
    for i, j in OFF_DIAGONAL:
        places[i, j] = row
        row += EDGES[i + 1] - EDGES[i]
    places["diagonal"] = row
    row += 8
    places["means"] = row
    row += 4 * tiles
    return places, -(-row // 32) * 32


def square_iotas():
    rows = lax.broadcasted_iota(jnp.int32, (BLOCK, BLOCK), 0)
    cols = lax.broadcasted_iota(jnp.int32, (BLOCK, BLOCK), 1)
    return rows, cols


def gram_kernel(tiles, where_ref, x_ref, send_ref, keep_ref, mean_ref, xs, pack):
    places, total = payload_rows(tiles)
    half = total // 2
    tile, line = where_ref[0], where_ref[1]
    parts = [x_ref[pl.ds(c, BANDS, stride=TILE_GROUPS), :] for c in range(TILE_GROUPS)]
    mean = jnp.sum(sum(parts[1:], parts[0]), axis=1, keepdims=True) / COUNT
    mean_ref[...] = jnp.broadcast_to(mean, (BANDS, LANES))
    for c in range(TILE_GROUPS):
        for k, part in enumerate(split3(parts[c] - mean)):
            xs[k, 0:BANDS, c * LANES : (c + 1) * LANES] = part
    xs[:, BANDS:, :] = jnp.zeros_like(xs[:, BANDS:, :])
    rows, cols = square_iotas()

    def rows_of(i):
        return [xs[k, 2 * i * BLOCK : 2 * (i + 1) * BLOCK, :] for k in range(3)]

    blocks = {}
    for i, j in ((0, 0), (1, 0), (1, 1)):
        square = product_parts(rows_of(i), rows_of(j), 1, 1)
        for a in range(2):
            for b in range(2):
                blocks[2 * i + a, 2 * j + b] = square[
                    a * BLOCK : (a + 1) * BLOCK, b * BLOCK : (b + 1) * BLOCK
                ]
    pack[places["diagonal"] :, :] = jnp.zeros_like(pack[places["diagonal"] :, :])
    for k in range(2):
        lower, upper = blocks[2 * k, 2 * k], blocks[2 * k + 1, 2 * k + 1]
        pack[k * BLOCK : (k + 1) * BLOCK, :] = jnp.where(rows >= cols, lower, upper)
        pack[places["diagonal"] + k : places["diagonal"] + k + 1, :] = jnp.sum(
            jnp.where(rows == cols, upper, 0.0), axis=0, keepdims=True
        )
    for i, j in OFF_DIAGONAL:
        height = EDGES[i + 1] - EDGES[i]
        pack[places[i, j] : places[i, j] + height, :] = blocks[i, j][:height]
    lane = lax.broadcasted_iota(jnp.int32, (BANDS, LANES), 1)
    mean_row = sum(
        lax.dot_general(
            jnp.ones((16, LANES), jnp.bfloat16),
            part,
            (((1,), (1,)), ((), ())),
            preferred_element_type=jnp.float32,
        )
        for part in split3(jnp.where(lane == 0, mean, 0.0))
    )
    which = lax.broadcasted_iota(jnp.int32, (tiles, BLOCK), 0)
    for c in range(4):
        width = EDGES[c + 1] - EDGES[c]
        place = places["means"] + c * tiles
        pack[place : place + tiles, 0:width] = jnp.where(
            which[:, :width] == tile, mean_row[0:1, EDGES[c] : EDGES[c + 1]], 0.0
        )
    keep_ref[...] = pack[pl.ds(pl.multiple_of(line * half, 8), half), :]
    send_ref[...] = pack[pl.ds(pl.multiple_of((1 - line) * half, 8), half), :]


def load_strip(where_ref, x_ref, other_ref, mean_ref, xs):
    mean = mean_ref[...]
    line = where_ref[1]
    for g in range(2 * TILE_GROUPS):
        if g < TILE_GROUPS:
            block = x_ref[pl.ds(g, BANDS, stride=TILE_GROUPS), :]
        else:
            k = g - TILE_GROUPS
            at = k + line * (TILE_GROUPS - 1 - 2 * k)
            block = other_ref[pl.ds(at, BANDS, stride=TILE_GROUPS), :]
        for k, part in enumerate(split3(block - mean)):
            xs[k, :, g * LANES : (g + 1) * LANES] = part


def strip_product(line_ref, samp_ref, xs, matrix, starts, depth):
    width = len(starts) * LANES

    def tiles_of(ref, rows):
        return jnp.concatenate([ref[rows, start : start + LANES] for start in starts], 1)

    samp = tiles_of(samp_ref, slice(None))
    for line in range(depth // SD):
        values = samp * tiles_of(line_ref, slice(line, line + 1))
        for k, part in enumerate(split3(values)):
            matrix[k, line * SD : (line + 1) * SD, 0:width] = part
    return product_parts(
        [xs[k, :, 0:depth] for k in range(3)], [matrix[k, 0:depth, 0:width] for k in range(3)], 1, 0
    )


def repacked(small, first, width):
    together = LANES // width
    height = BANDS // together
    lane = lax.broadcasted_iota(jnp.int32, (height, LANES), 1)
    result = jnp.zeros((height, LANES), jnp.float32)
    for k in range(together):
        taken = small[pl.ds(k, height, stride=together), :]
        moved = pltpu.roll(taken, (k * width - first) % LANES, 1)
        result = jnp.where((lane >= k * width) & (lane < (k + 1) * width), moved, result)
    return result


FAR_ROWS = BANDS * FAR // LANES
FAR_HELD = -(-FAR_ROWS // 8) * 8


NEAR_SHALLOW, NEAR_DEEP, FAR_AT = COUNT, COUNT + 2 * LANES, COUNT + 4 * LANES


def first_kernel(where_ref, x_ref, other_ref, mean_ref, line_ref, samp_ref, xs, near1, far, matrix, small):
    load_strip(where_ref, x_ref, other_ref, mean_ref, xs)
    run = functools.partial(strip_product, line_ref, samp_ref, xs, matrix)
    near1[:, 0:LANES] = run((NEAR_SHALLOW,), SHALLOW)
    deep = run((NEAR_DEEP, FAR_AT), 2 * COUNT)
    near1[:, LANES:] = deep[:, 0:LANES]
    small[...] = deep[:, LANES:]
    far[FAR_ROWS:, :] = jnp.zeros_like(far[FAR_ROWS:, :])
    far[0:FAR_ROWS, :] = repacked(small, 0, FAR)


def second_kernel(xs, line_ref, samp_ref, near2, own_deep, matrix):
    run = functools.partial(strip_product, line_ref, samp_ref, xs, matrix)
    near2[:, 0:LANES] = run((NEAR_SHALLOW + LANES,), SHALLOW)
    deep = run((NEAR_DEEP + LANES, LEVEL1), 2 * COUNT)
    near2[:, LANES:] = deep[:, 0:LANES]
    own_deep[...] = deep[:, LANES:]


def third_kernel(xs, line_ref, samp_ref, own_shallow, matrix):
    run = functools.partial(strip_product, line_ref, samp_ref, xs, matrix)
    own_shallow[...] = run(tuple(range(0, LEVEL1, LANES)), SHALLOW)


def spread(value):
    return jnp.broadcast_to(value, (8, LANES))


def added(terms):
    terms = list(terms)
    while len(terms) > 1:
        terms = [sum(terms[k + 1 : k + 2], terms[k]) for k in range(0, len(terms), 2)]
    return terms[0]


NEAR = 2


def inverse_factor(groups, held):
    rows = list(groups)
    lane = lax.broadcasted_iota(jnp.int32, (8, LANES), 1)
    sub = lax.broadcasted_iota(jnp.int32, (8, LANES), 0)
    done = []

    def columns(group, base):
        return [spread(group[:, base + t : base + t + 1]) for t in range(8)]

    following = columns(rows[0], 0)
    for b in range(len(rows)):
        base, slot = 8 * b, b % 2
        current = rows[b]
        for t in range(8):
            held[slot, t] = following[t]
        s = [[spread(held[slot, t, u : u + 1, :]) if u >= t else None for t in range(8)] for u in range(8)]
        inside = (lane >= base) & (lane < base + 8)
        start = jnp.where(inside, jnp.where(lane == base + sub, 1.0, 0.0), current)
        y = [spread(start[t : t + 1, :]) for t in range(8)]
        near = list(range(b + 1, min(len(rows), b + 1 + NEAR)))
        far = list(range(b + 1 + NEAR, len(rows)))
        g = {i: columns(rows[i], base) for i in near}
        if near:
            raw = columns(rows[b + 1], base + 8)
        r = [None] * 8
        l = [[None] * 8 for _ in range(8)]
        for p in range(8):
            r[p] = pl.reciprocal(s[p][p], approx=True)
            for t in range(p + 1, 8):
                l[t][p] = s[t][p] * r[p]
            for t in range(p + 1, 8):
                for u in range(t, 8):
                    if u == t == p + 1:
                        s[u][t] = s[u][t] - (s[u][p] * s[t][p]) * r[p]
                    else:
                        s[u][t] = s[u][t] - s[u][p] * l[t][p]
                for i in near:
                    g[i][t] = g[i][t] - g[i][p] * l[t][p]
                y[t] = y[t] - l[t][p] * y[p]
        scaled = {i: [g[i][p] * r[p] for p in range(8)] for i in near}
        if near:
            for p in range(8):
                held[slot, 8 + p] = scaled[b + 1][p]
            following = [
                raw[t] - added(g[b + 1][p] * spread(held[slot, 8 + p, t : t + 1, :]) for p in range(8))
                for t in range(8)
            ]
        for i in near:
            rows[i] = jnp.where(inside, 0.0, rows[i]) - added(scaled[i][p] * y[p] for p in range(8))
        if far:
            z = [None] * 8
            for t in range(7, -1, -1):
                z[t] = r[t] * y[t]
                for u in range(t + 1, 8):
                    z[t] = z[t] - l[u][t] * z[u]
            for i in far:
                old = columns(rows[i], base)
                rows[i] = jnp.where(inside, 0.0, rows[i]) - added(old[t] * z[t] for t in range(8))
        q, d = y[0], s[0][0]
        for t in range(1, 8):
            q = jnp.where(sub == t, y[t], q)
            d = jnp.where(sub == t, s[t][t], d)
        done.append(jnp.where(lane < base + 8, q * lax.rsqrt(d), 0.0))
    return done


def whiten_kernel(tiles, where_ref, mine_ref, theirs_ref, w_ref, dev_ref, pack, a, held):
    places, total = payload_rows(tiles)
    half = total // 2
    line = where_ref[1]
    pack[pl.ds(pl.multiple_of(line * half, 8), half), :] = mine_ref[...]
    pack[pl.ds(pl.multiple_of((1 - line) * half, 8), half), :] = theirs_ref[...]
    at = places["means"]
    means = jnp.concatenate([pack[at + c * tiles : at + (c + 1) * tiles, :] for c in range(4)], 1)
    dev = means - jnp.sum(means, axis=0, keepdims=True) / tiles
    dev_ref[...] = dev
    between = (LD * SD) * product(dev, dev, 0, 0)
    rows, cols = square_iotas()
    trace = jnp.zeros((1, BLOCK), jnp.float32)
    for k in range(2):
        packed = pack[k * BLOCK : (k + 1) * BLOCK, :]
        turned = packed.T
        diagonal = pack[places["diagonal"] + k : places["diagonal"] + k + 1, :]
        lower = jnp.where(rows >= cols, packed, turned)
        upper = jnp.where(rows < cols, packed, jnp.where(rows > cols, turned, diagonal))
        for i, full in ((2 * k, lower), (2 * k + 1, upper)):
            low, high = EDGES[i], EDGES[i + 1]
            full = full + between[i * BLOCK : (i + 1) * BLOCK, i * BLOCK : (i + 1) * BLOCK]
            trace += jnp.sum(jnp.where(rows == cols, full, 0.0), axis=0, keepdims=True)
            a[low:high, i * BLOCK : (i + 1) * BLOCK] = full[: high - low]
    for i, j in OFF_DIAGONAL:
        low, high = EDGES[i], EDGES[i + 1]
        a[low:high, j * BLOCK : (j + 1) * BLOCK] = (
            pack[places[i, j] : places[i, j] + high - low, :]
            + between[low:high, j * BLOCK : (j + 1) * BLOCK]
        )
    load = 0.01 * (jnp.sum(trace, axis=1, keepdims=True) / BANDS)
    for i in range(4):
        low, high = EDGES[i], EDGES[i + 1]
        full = a[low:high, i * BLOCK : (i + 1) * BLOCK]
        height = high - low
        a[low:high, i * BLOCK : (i + 1) * BLOCK] = full + jnp.where(
            (rows == cols)[:height], load, 0.0
        )
    w_ref[...] = jnp.zeros_like(w_ref)
    for k in range(4):
        low, high = EDGES[k], EDGES[k + 1]
        groups = [a[low + 8 * g : low + 8 * g + 8, low : low + BLOCK] for g in range((high - low) // 8)]
        m = jnp.concatenate(inverse_factor(groups, held), 0)[:, : high - low]
        if k:
            w_ref[low:high, :low] = product(m, w_ref[low:high, :low], 1, 0)
        w_ref[low:high, low:high] = m
        if high < BANDS:
            parts = split3(m)
            factor = split3(product_parts(split3(a[high:, low:high]), parts, 1, 1))
            a[high:, high:BANDS] = a[high:, high:BANDS] - product_parts(factor, factor, 1, 1)
            w_ref[high:, :high] = w_ref[high:, :high] - product_parts(factor, split3(w_ref[low:high, :high]), 1, 0)


def output_kernel(
    n_line, pixels, where_ref, own_ref, deep_ref, dev_ref, w_ref, offset_ref, select_ref, near1, near2, far_ref, *rest
):
    (out1_ref, out2_ref, out3_ref, approx_ref), (d, small) = rest[:4], rest[4:]
    tile, samp = where_ref[0], where_ref[2]
    bit = samp % 2
    tiles = dev_ref.shape[0]
    which = lax.broadcasted_iota(jnp.int32, (tiles, COUNT), 0)
    near = 1 - 2 * bit
    gains = jnp.where(which == tile, offset_ref[4:5, :], 0.0)
    for k, step in enumerate((near, -near, 2 * near, -2 * near)):
        gains += jnp.where(which == tile + n_line * step, offset_ref[k : k + 1, :], 0.0)
    shift = product(dev_ref[:, 0:BANDS], gains, 0, 0)
    together = LANES // FAR
    lane = lax.broadcasted_iota(jnp.int32, (FAR_ROWS, LANES), 1)
    for k in range(together):
        moved = pltpu.roll(far_ref[0:FAR_ROWS, :], LANES - FAR - k * FAR, 1)
        small[pl.ds(k, FAR_ROWS, stride=together), :] = jnp.where(lane >= LANES - FAR, moved, 0.0)
    lane = lax.broadcasted_iota(jnp.int32, (BANDS, LANES), 1) % WIDE
    scale = float(pixels) ** 0.5

    def keep(at, value):
        for k, part in enumerate(split3(value * scale)):
            d[k, :, at : at + LANES] = part

    deep = split3(jnp.concatenate([near1[:, LANES:], near2[:, LANES:]], 1))
    select = select_ref[...].astype(jnp.bfloat16)
    near_deep = lax.dot_general(
        jnp.concatenate(deep, 1),
        jnp.concatenate([select] * 3, 0),
        (((1,), (0,)), ((), ())),
        preferred_element_type=jnp.float32,
    )
    bases = ((WIDE - 2) * (1 - bit), (WIDE - 2) * bit)
    for sb in range(3):
        at = sb * LANES
        value = own_ref[:, at : at + LANES] + shift[:, at : at + LANES]
        for base, ref in zip(bases, (near1, near2)):
            moved = pltpu.roll(ref[:, 0:LANES], (base - 2 * sb + LANES) % LANES, 1)
            value += jnp.where((lane >= base) & (lane < base + 2), moved, 0.0)
        keep(at, value)
    keep(
        LEVEL1,
        deep_ref[...] + shift[:, LEVEL1:] + near_deep + small[...],
    )
    for low, high in ((0, 2 * BLOCK), (2 * BLOCK, BANDS)):
        w = split3(w_ref[low:high, :high])
        out = product_parts(w, [d[k, 0:high, :] for k in range(3)], 1, 0)
        for sb in range(3):
            out1_ref[sb * BANDS + low : sb * BANDS + high, :] = out[:, sb * LANES : (sb + 1) * LANES]
        small[low:high, :] = out[:, LEVEL1:]
    size2, size3 = COUNT // 16, COUNT // 64
    rows2, rows3 = BANDS * size2 // LANES, BANDS * size3 // LANES
    for sb in range(3):
        out2_ref[sb * rows2 : (sb + 1) * rows2, :] = repacked(small, sb * size2, size2)
        out3_ref[sb * rows3 : (sb + 1) * rows3, :] = repacked(small, 3 * size2 + sb * size3, size3)
    approx_ref[...] = repacked(small, 3 * size2 + 3 * size3, size3)


def permuted(array, axis, partner):
    count = lax.axis_size(axis)
    return lax.ppermute(array, axis, [(i, partner(i)) for i in range(count) if 0 <= partner(i) < count])


def mirrored(size):
    def partner(i):
        within = i % size
        return i - within + 2 * (size // 2 - 1 - within // 2) + within % 2

    return partner


VMEM = pl.BlockSpec(memory_space=pltpu.VMEM)
SMEM = pl.BlockSpec(memory_space=pltpu.SMEM)


def call(kernel, name, shapes, inputs, scratch, flops):
    specs = [SMEM if value.dtype == jnp.int32 and value.ndim == 1 else VMEM for value in inputs]
    size = sum(value.size * 4 for value in inputs)
    return pl.pallas_call(
        kernel,
        name=name,
        out_shape=[
            shape if isinstance(shape, jax.ShapeDtypeStruct) else jax.ShapeDtypeStruct(shape, jnp.float32)
            for shape in shapes
        ],
        in_specs=specs,
        out_specs=[VMEM] * len(shapes),
        scratch_shapes=[pltpu.VMEM(shape, dtype) for shape, dtype in scratch],
        compiler_params=pltpu.CompilerParams(vmem_limit_bytes=16 * 2**20),
        cost_estimate=pl.CostEstimate(flops=flops, bytes_accessed=size, transcendentals=0),
    )(*inputs)


def local(constants, cube):
    line_table, samp_table, offset_table, select_table, relayed = (jnp.asarray(table) for table in constants)
    n_samp, n_line = lax.axis_size("samp"), lax.axis_size("line")
    tiles = n_samp * n_line
    samp, line = lax.axis_index("samp"), lax.axis_index("line")
    where = jnp.stack([samp * n_line + line, line, samp]).astype(jnp.int32)
    f32, bf16 = jnp.float32, jnp.bfloat16
    x = cube.reshape(BANDS * COUNT // LANES, LANES)
    other = permuted(x, "line", lambda i: i ^ 1)
    _, total = payload_rows(tiles)
    half, quarter = total // 2, total // 4
    lines, samps = line_table[line, samp & 1], samp_table[samp]
    offset, select = offset_table[samp, line], select_table[samp & 1]
    x, lines = lax.optimization_barrier((x, lines))
    send, keep, mean = call(
        functools.partial(gram_kernel, tiles),
        "gram",
        [(half, LANES), (half, LANES), (BANDS, LANES)],
        [where, x],
        [((3, 4 * BLOCK, COUNT), bf16), ((total, LANES), f32)],
        2 * BANDS * BANDS * COUNT * 4,
    )
    summed = keep + permuted(send, "line", lambda i: i ^ 1)
    side = ((samp >> 1) ^ (samp >> 2)) & 1
    kept = lax.dynamic_slice_in_dim(summed, side * quarter, quarter, 0)
    given = lax.dynamic_slice_in_dim(summed, (1 - side) * quarter, quarter, 0)

    mean, given, other, samps = lax.optimization_barrier((mean, given, other, samps))
    strip, near1, far = call(
        first_kernel,
        "first",
        [jax.ShapeDtypeStruct((3, BANDS, 2 * COUNT), bf16), (BANDS, 2 * LANES), (FAR_HELD, LANES)],
        [where, x, other, mean, lines, samps],
        [((3, 2 * COUNT, 2 * LANES), bf16), ((BANDS, LANES), f32)],
        2 * BANDS * 2 * COUNT * 3 * LANES * 6,
    )
    kept = kept + permuted(given, "samp", lambda i: i ^ 2)
    kept, near1, far, strip = lax.optimization_barrier((kept, near1, far, strip))
    near2, own_deep = call(
        second_kernel,
        "second",
        [(BANDS, 2 * LANES), (BANDS, LANES)],
        [strip, lines, samps],
        [((3, 2 * COUNT, 2 * LANES), bf16)],
        2 * BANDS * 2 * COUNT * 3 * LANES * 6,
    )
    kept = kept + permuted(kept, "samp", lambda i: i ^ 1)
    kept, near1, near2, own_deep, far, strip = lax.optimization_barrier(
        (kept, near1, near2, own_deep, far, strip)
    )
    near1 = permuted(near1, "samp", lambda i: i ^ 1)
    (own,) = call(
        third_kernel,
        "third",
        [(BANDS, LEVEL1)],
        [strip, lines, samps],
        [((3, SHALLOW, LEVEL1), bf16)],
        2 * BANDS * 2 * COUNT * 3 * LANES * 6,
    )
    size = 8
    while size <= n_samp:
        kept = kept + permuted(kept, "samp", mirrored(size))
        size *= 2
    kept, own, far, offset, select = lax.optimization_barrier((kept, own, far, offset, select))
    far = permuted(far, "samp", lambda i: i + 2 if i & 1 else i - 2)
    back = permuted(kept, "samp", lambda i: i ^ 2)
    mine = jnp.where(side == 0, jnp.concatenate([kept, back]), jnp.concatenate([back, kept]))
    mine, near1 = lax.optimization_barrier((mine, near1))
    theirs = permuted(mine, "line", lambda i: i ^ 1)
    on = jnp.concatenate([jnp.zeros_like(relayed), relayed], 2)[1 - (samp & 1)]
    near2 = permuted(jnp.where(on, near1, near2), "samp", lambda i: ((i + 1) ^ 1) - 1)

    w, dev = call(
        functools.partial(whiten_kernel, tiles),
        "whiten",
        [(BANDS, BANDS), (tiles, 4 * BLOCK)],
        [where, mine, theirs],
        [((total, LANES), f32), ((BANDS, 4 * BLOCK), f32), ((2, 16, 8, LANES), f32)],
        10**8,
    )
    outs = call(
        functools.partial(output_kernel, n_line, COUNT * tiles),
        "outputs",
        [
            (3 * BANDS * (COUNT // 4) // LANES, LANES),
            (3 * BANDS * (COUNT // 16) // LANES, LANES),
            (3 * BANDS * (COUNT // 64) // LANES, LANES),
            (BANDS * (COUNT // 64) // LANES, LANES),
        ],
        [where, own, own_deep, dev, w, offset, select, near1, near2, far],
        [((3, BANDS, COUNT), bf16), ((BANDS, LANES), f32)],
        2 * BANDS * BANDS * COUNT * 6,
    )
    return tuple(out.reshape(-1) for out in outs)


def solution(mesh):
    n_samp, n_line = mesh.shape["samp"], mesh.shape["line"]
    assert n_line == 2 and n_samp >= 8 and n_samp & (n_samp - 1) == 0
    constants = build_constants(n_samp, n_line)
    spec = P(("groups", "samp", "line"))
    return jax.shard_map(
        functools.partial(local, constants),
        mesh=mesh,
        in_specs=(spec,),
        out_specs=(spec,) * 4,
        check_vma=False,
    )
```

```python
import functools

import numpy as np
import jax
import jax.numpy as jnp
from jax import lax
from jax.experimental import pallas as pl
from jax.experimental.pallas import tpu as pltpu
from jax.sharding import PartitionSpec as P

BANDS = 432
LD = 32
SD = 16
LANES = 128
BLOCK = 128

alpha_lift = -1.586134342059924
beta_lift = -0.052980118572961
gamma_lift = 0.882911075530934
delta_lift = 0.443506852043971
scale_lift = 1.230174104914001


def split3(value):
    high = value.astype(jnp.bfloat16)
    rest = value - high.astype(jnp.float32)
    middle = rest.astype(jnp.bfloat16)
    return high, middle, (rest - middle.astype(jnp.float32)).astype(jnp.bfloat16)


def left_terms(parts, dim):
    high, middle, low = parts
    return jnp.concatenate([high, high, middle, high, low, middle], dim)


def right_terms(parts, dim):
    high, middle, low = parts
    return jnp.concatenate([high, middle, high, low, high, middle], dim)


def product_parts(left, right, left_dim, right_dim):
    return lax.dot_general(
        left_terms(left, left_dim),
        right_terms(right, right_dim),
        (((left_dim,), (right_dim,)), ((), ())),
        preferred_element_type=jnp.float32,
    )


def product(left, right, left_dim, right_dim):
    return product_parts(split3(left), split3(right), left_dim, right_dim)


def lift_rows(values):
    evens, odds = values[0::2], values[1::2]
    for weight_odd, weight_even in ((alpha_lift, beta_lift), (gamma_lift, delta_lift)):
        following = np.concatenate([evens[1:], evens[-1:]])
        odds = odds + weight_odd * (evens + following)
        preceding = np.concatenate([odds[:1], odds[:-1]])
        evens = evens + weight_even * (preceding + odds)
    return evens / scale_lift, odds * scale_lift


def axis_operators(length):
    operators = {}
    current = np.eye(length)
    for level in (1, 2, 3):
        low, high = lift_rows(current)
        operators[level, 0], operators[level, 1] = low, high
        current = low
    return operators


def output_lanes():
    lanes = []
    for level in (1, 2, 3):
        parts = [(1, 0), (0, 1), (1, 1)] + ([(0, 0)] if level == 3 else [])
        for line_part, samp_part in parts:
            for line in range(LD >> level):
                for samp in range(SD >> level):
                    lanes.append((level, line_part, samp_part, line, samp))
    return lanes


GROUP = LANES // SD
TILE_GROUPS = LD // GROUP
SHALLOW = (TILE_GROUPS + 1) * LANES
WIDE = SD // 2
LEVEL1 = 3 * (LD // 2) * WIDE
COUNT = LD * SD
FAR = COUNT // 16


def strip_lines(q):
    own = list(range(q * LD, (q + 1) * LD))
    groups = [list(range((1 - q) * LD + g * GROUP, (1 - q) * LD + (g + 1) * GROUP)) for g in range(TILE_GROUPS)]
    if q == 1:
        groups = groups[::-1]
    return own + [line for group in groups for line in group]


def neighbour_steps(p):
    near = 1 - 2 * (p & 1)
    return near, -near, 2 * near, -2 * near


def relay_lanes(samp_ops, n_samp):
    lanes = output_lanes()
    pairs = []
    for parity in range(2):
        used = np.zeros((2, COUNT), bool)
        for p in range(n_samp):
            for k, step in enumerate((1 - 2 * parity, 2 - 4 * parity)):
                if 0 <= p + step < n_samp:
                    for o, (level, _, part, _, samp) in enumerate(lanes):
                        row = samp_ops[level, part][(p + step) * (SD >> level) + samp]
                        used[k, o] |= row[p * SD : (p + 1) * SD].any()
        free = [o - LEVEL1 for o in range(LEVEL1, COUNT) if not used[0, o]]
        wanted = [o for o in range(COUNT) if used[1, o]]
        assert len(wanted) <= len(free)
        pairs.append(list(zip(free, wanted)))
    return pairs


def build_constants(n_samp, n_line):
    lanes = output_lanes()
    line_ops = axis_operators(LD * n_line)
    samp_ops = axis_operators(SD * n_samp)
    line_own = np.zeros((n_line, n_line * LD, COUNT))
    for q in range(n_line):
        order = strip_lines(q)
        for o, (level, part, _, line, _) in enumerate(lanes):
            line_own[q, :, o] = line_ops[level, part][q * (LD >> level) + line][order]
    assert not line_own[:, SHALLOW // SD :, :LEVEL1].any()

    def reach(p, step):
        table = np.zeros((SD, COUNT))
        if 0 <= p + step < n_samp:
            for o, (level, _, part, _, samp) in enumerate(lanes):
                row = samp_ops[level, part][(p + step) * (SD >> level) + samp]
                table[:, o] = row[p * SD : (p + 1) * SD]
        return table

    size = COUNT + 5 * LANES
    relays = relay_lanes(samp_ops, n_samp)
    select = np.zeros((2, 2 * LANES, LANES))
    for parity in range(2):
        passed, moved = dict(relays[1 - parity]), dict(relays[parity])
        for lane in range(LANES):
            select[parity, lane, lane] = float(lane not in passed)
            select[parity, LANES + lane, moved[lane] - LEVEL1 if lane in moved else lane] = 1.0
    line_table = np.zeros((n_line, n_line * LD, size))
    samp_table = np.zeros((n_samp, SD, size))
    line_table[:, :, :COUNT] = line_own
    for k in range(2):
        at = COUNT + k * LANES
        for line in range(LD // 2):
            for sb in range(3):
                for j in range(2):
                    source = (sb * (LD // 2) + line) * WIDE
                    line_table[:, :, at + line * WIDE + 2 * sb + j] = line_own[:, :, source]
        at = COUNT + (2 + k) * LANES
        line_table[:, :, at : at + LANES] = line_own[:, :, LEVEL1:]
    at = COUNT + 4 * LANES
    line_table[:, :, at : at + FAR] = line_own[:, :, COUNT - FAR :]
    line_table = np.stack([line_table] * 2, 1)
    for parity in range(2):
        for lane, o in relays[parity]:
            line_table[:, parity, :, COUNT + 2 * LANES + lane] = line_own[:, :, o]
    offsets = np.zeros((n_samp, n_line, 8, COUNT))
    line_sums = line_own.sum(1)
    for p in range(n_samp):
        samp_table[p, :, :COUNT] = reach(p, 0)
        whole = reach(p, 0).sum(0)
        for k, step in enumerate(neighbour_steps(p)):
            given = reach(p, step)
            if k < 2:
                base = 0 if step > 0 else WIDE - 2
                left = given.copy()
                for line in range(LD // 2):
                    for sb in range(3):
                        for j in range(2):
                            source = (sb * (LD // 2) + line) * WIDE + base + j
                            samp_table[p, :, COUNT + k * LANES + line * WIDE + 2 * sb + j] = given[:, source]
                            left[:, source] = 0.0
                assert not left[:, :LEVEL1].any()
                at = COUNT + (2 + k) * LANES
                samp_table[p, :, at : at + LANES] = given[:, LEVEL1:]
            else:
                assert not given[:, : COUNT - FAR].any()
                if k == 2:
                    for lane, o in relays[p % 2]:
                        samp_table[p, :, COUNT + 2 * LANES + lane] = given[:, o]
                else:
                    at = COUNT + 4 * LANES
                    samp_table[p, :, at : at + FAR] = given[:, COUNT - FAR :]
            if 0 <= p + step < n_samp:
                sums = reach(p + step, -step).sum(0)
                offsets[p, :, k] = sums * line_sums
                whole = whole + sums
        offsets[p, :, 4] = whole * line_sums
        offsets[p, :, 4] -= offsets[p, :, :4].sum(1)
    relayed = np.zeros((2, 1, LANES), bool)
    for parity in range(2):
        relayed[parity, 0, [lane for lane, _ in relays[parity]]] = True
    return (
        line_table.astype(np.float32),
        samp_table.astype(np.float32),
        offsets.astype(np.float32),
        select.astype(np.float32),
        relayed,
    )


EDGES = list(range(0, BANDS, BLOCK)) + [BANDS]
LAST = EDGES[-1] - EDGES[-2]
OFF_DIAGONAL = ((1, 0), (2, 0), (2, 1), (3, 0), (3, 1), (3, 2))


def payload_rows(tiles):
    places = {}
    row = 2 * BLOCK
    for i, j in OFF_DIAGONAL:
        places[i, j] = row
        row += EDGES[i + 1] - EDGES[i]
    places["diagonal"] = row
    row += 8
    places["means"] = row
    row += 4 * tiles
    return places, -(-row // 32) * 32


def square_iotas():
    rows = lax.broadcasted_iota(jnp.int32, (BLOCK, BLOCK), 0)
    cols = lax.broadcasted_iota(jnp.int32, (BLOCK, BLOCK), 1)
    return rows, cols


def gram_kernel(tiles, where_ref, x_ref, send_ref, keep_ref, mean_ref, xs, pack):
    places, total = payload_rows(tiles)
    half = total // 2
    tile, line = where_ref[0], where_ref[1]
    parts = [x_ref[pl.ds(c, BANDS, stride=TILE_GROUPS), :] for c in range(TILE_GROUPS)]
    mean = jnp.sum(sum(parts[1:], parts[0]), axis=1, keepdims=True) / COUNT
    mean_ref[...] = jnp.broadcast_to(mean, (BANDS, LANES))
    for c in range(TILE_GROUPS):
        for k, part in enumerate(split3(parts[c] - mean)):
            xs[k, 0:BANDS, c * LANES : (c + 1) * LANES] = part
    xs[:, BANDS:, :] = jnp.zeros_like(xs[:, BANDS:, :])
    rows, cols = square_iotas()

    def rows_of(i):
        return [xs[k, 2 * i * BLOCK : 2 * (i + 1) * BLOCK, :] for k in range(3)]

    blocks = {}
    for i, j in ((0, 0), (1, 0), (1, 1)):
        square = product_parts(rows_of(i), rows_of(j), 1, 1)
        for a in range(2):
            for b in range(2):
                blocks[2 * i + a, 2 * j + b] = square[
                    a * BLOCK : (a + 1) * BLOCK, b * BLOCK : (b + 1) * BLOCK
                ]
    pack[places["diagonal"] :, :] = jnp.zeros_like(pack[places["diagonal"] :, :])
    for k in range(2):
        lower, upper = blocks[2 * k, 2 * k], blocks[2 * k + 1, 2 * k + 1]
        pack[k * BLOCK : (k + 1) * BLOCK, :] = jnp.where(rows >= cols, lower, upper)
        pack[places["diagonal"] + k : places["diagonal"] + k + 1, :] = jnp.sum(
            jnp.where(rows == cols, upper, 0.0), axis=0, keepdims=True
        )
    for i, j in OFF_DIAGONAL:
        height = EDGES[i + 1] - EDGES[i]
        pack[places[i, j] : places[i, j] + height, :] = blocks[i, j][:height]
    lane = lax.broadcasted_iota(jnp.int32, (BANDS, LANES), 1)
    mean_row = sum(
        lax.dot_general(
            jnp.ones((16, LANES), jnp.bfloat16),
            part,
            (((1,), (1,)), ((), ())),
            preferred_element_type=jnp.float32,
        )
        for part in split3(jnp.where(lane == 0, mean, 0.0))
    )
    which = lax.broadcasted_iota(jnp.int32, (tiles, BLOCK), 0)
    for c in range(4):
        width = EDGES[c + 1] - EDGES[c]
        place = places["means"] + c * tiles
        pack[place : place + tiles, 0:width] = jnp.where(
            which[:, :width] == tile, mean_row[0:1, EDGES[c] : EDGES[c + 1]], 0.0
        )
    keep_ref[...] = pack[pl.ds(pl.multiple_of(line * half, 8), half), :]
    send_ref[...] = pack[pl.ds(pl.multiple_of((1 - line) * half, 8), half), :]


def load_strip(where_ref, x_ref, other_ref, mean_ref, xs):
    mean = mean_ref[...]
    line = where_ref[1]
    for g in range(2 * TILE_GROUPS):
        if g < TILE_GROUPS:
            block = x_ref[pl.ds(g, BANDS, stride=TILE_GROUPS), :]
        else:
            k = g - TILE_GROUPS
            at = k + line * (TILE_GROUPS - 1 - 2 * k)
            block = other_ref[pl.ds(at, BANDS, stride=TILE_GROUPS), :]
        for k, part in enumerate(split3(block - mean)):
            xs[k, :, g * LANES : (g + 1) * LANES] = part


def strip_product(line_ref, samp_ref, xs, matrix, starts, depth):
    width = len(starts) * LANES

    def tiles_of(ref, rows):
        return jnp.concatenate([ref[rows, start : start + LANES] for start in starts], 1)

    samp = tiles_of(samp_ref, slice(None))
    for line in range(depth // SD):
        values = samp * tiles_of(line_ref, slice(line, line + 1))
        for k, part in enumerate(split3(values)):
            matrix[k, line * SD : (line + 1) * SD, 0:width] = part
    return product_parts(
        [xs[k, :, 0:depth] for k in range(3)], [matrix[k, 0:depth, 0:width] for k in range(3)], 1, 0
    )


def repacked(small, first, width):
    together = LANES // width
    height = BANDS // together
    lane = lax.broadcasted_iota(jnp.int32, (height, LANES), 1)
    result = jnp.zeros((height, LANES), jnp.float32)
    for k in range(together):
        taken = small[pl.ds(k, height, stride=together), :]
        moved = pltpu.roll(taken, (k * width - first) % LANES, 1)
        result = jnp.where((lane >= k * width) & (lane < (k + 1) * width), moved, result)
    return result


FAR_ROWS = BANDS * FAR // LANES
FAR_HELD = -(-FAR_ROWS // 8) * 8


NEAR_SHALLOW, NEAR_DEEP, FAR_AT = COUNT, COUNT + 2 * LANES, COUNT + 4 * LANES


def first_kernel(where_ref, x_ref, other_ref, mean_ref, line_ref, samp_ref, xs, near1, far, matrix, small):
    load_strip(where_ref, x_ref, other_ref, mean_ref, xs)
    run = functools.partial(strip_product, line_ref, samp_ref, xs, matrix)
    near1[:, 0:LANES] = run((NEAR_SHALLOW,), SHALLOW)
    deep = run((NEAR_DEEP, FAR_AT), 2 * COUNT)
    near1[:, LANES:] = deep[:, 0:LANES]
    small[...] = deep[:, LANES:]
    far[FAR_ROWS:, :] = jnp.zeros_like(far[FAR_ROWS:, :])
    far[0:FAR_ROWS, :] = repacked(small, 0, FAR)


def second_kernel(xs, line_ref, samp_ref, near2, own_deep, matrix):
    run = functools.partial(strip_product, line_ref, samp_ref, xs, matrix)
    near2[:, 0:LANES] = run((NEAR_SHALLOW + LANES,), SHALLOW)
    deep = run((NEAR_DEEP + LANES, LEVEL1), 2 * COUNT)
    near2[:, LANES:] = deep[:, 0:LANES]
    own_deep[...] = deep[:, LANES:]


def third_kernel(xs, line_ref, samp_ref, own_shallow, matrix):
    run = functools.partial(strip_product, line_ref, samp_ref, xs, matrix)
    own_shallow[...] = run(tuple(range(0, LEVEL1, LANES)), SHALLOW)


def spread(value):
    return jnp.broadcast_to(value, (8, LANES))


def added(terms):
    terms = list(terms)
    while len(terms) > 1:
        terms = [sum(terms[k + 1 : k + 2], terms[k]) for k in range(0, len(terms), 2)]
    return terms[0]


NEAR = 2


def inverse_factor(groups, held):
    rows = list(groups)
    lane = lax.broadcasted_iota(jnp.int32, (8, LANES), 1)
    sub = lax.broadcasted_iota(jnp.int32, (8, LANES), 0)
    done = []

    def columns(group, base):
        return [spread(group[:, base + t : base + t + 1]) for t in range(8)]

    following = columns(rows[0], 0)
    for b in range(len(rows)):
        base, slot = 8 * b, b % 2
        current = rows[b]
        for t in range(8):
            held[slot, t] = following[t]
        s = [[spread(held[slot, t, u : u + 1, :]) if u >= t else None for t in range(8)] for u in range(8)]
        inside = (lane >= base) & (lane < base + 8)
        start = jnp.where(inside, jnp.where(lane == base + sub, 1.0, 0.0), current)
        y = [spread(start[t : t + 1, :]) for t in range(8)]
        near = list(range(b + 1, min(len(rows), b + 1 + NEAR)))
        far = list(range(b + 1 + NEAR, len(rows)))
        g = {i: columns(rows[i], base) for i in near}
        if near:
            raw = columns(rows[b + 1], base + 8)
        r = [None] * 8
        l = [[None] * 8 for _ in range(8)]
        for p in range(8):
            r[p] = pl.reciprocal(s[p][p], approx=True)
            for t in range(p + 1, 8):
                l[t][p] = s[t][p] * r[p]
            for t in range(p + 1, 8):
                for u in range(t, 8):
                    if u == t == p + 1:
                        s[u][t] = s[u][t] - (s[u][p] * s[t][p]) * r[p]
                    else:
                        s[u][t] = s[u][t] - s[u][p] * l[t][p]
                for i in near:
                    g[i][t] = g[i][t] - g[i][p] * l[t][p]
                y[t] = y[t] - l[t][p] * y[p]
        scaled = {i: [g[i][p] * r[p] for p in range(8)] for i in near}
        if near:
            for p in range(8):
                held[slot, 8 + p] = scaled[b + 1][p]
            following = [
                raw[t] - added(g[b + 1][p] * spread(held[slot, 8 + p, t : t + 1, :]) for p in range(8))
                for t in range(8)
            ]
        for i in near:
            rows[i] = jnp.where(inside, 0.0, rows[i]) - added(scaled[i][p] * y[p] for p in range(8))
        if far:
            z = [None] * 8
            for t in range(7, -1, -1):
                z[t] = r[t] * y[t]
                for u in range(t + 1, 8):
                    z[t] = z[t] - l[u][t] * z[u]
            for i in far:
                old = columns(rows[i], base)
                rows[i] = jnp.where(inside, 0.0, rows[i]) - added(old[t] * z[t] for t in range(8))
        q, d = y[0], s[0][0]
        for t in range(1, 8):
            q = jnp.where(sub == t, y[t], q)
            d = jnp.where(sub == t, s[t][t], d)
        done.append(jnp.where(lane < base + 8, q * lax.rsqrt(d), 0.0))
    return done


def whiten_kernel(tiles, where_ref, mine_ref, theirs_ref, w_ref, dev_ref, pack, a, held):
    places, total = payload_rows(tiles)
    half = total // 2
    line = where_ref[1]
    pack[pl.ds(pl.multiple_of(line * half, 8), half), :] = mine_ref[...]
    pack[pl.ds(pl.multiple_of((1 - line) * half, 8), half), :] = theirs_ref[...]
    at = places["means"]
    means = jnp.concatenate([pack[at + c * tiles : at + (c + 1) * tiles, :] for c in range(4)], 1)
    dev = means - jnp.sum(means, axis=0, keepdims=True) / tiles
    dev_ref[...] = dev
    between = (LD * SD) * product(dev, dev, 0, 0)
    rows, cols = square_iotas()
    trace = jnp.zeros((1, BLOCK), jnp.float32)
    for k in range(2):
        packed = pack[k * BLOCK : (k + 1) * BLOCK, :]
        turned = packed.T
        diagonal = pack[places["diagonal"] + k : places["diagonal"] + k + 1, :]
        lower = jnp.where(rows >= cols, packed, turned)
        upper = jnp.where(rows < cols, packed, jnp.where(rows > cols, turned, diagonal))
        for i, full in ((2 * k, lower), (2 * k + 1, upper)):
            low, high = EDGES[i], EDGES[i + 1]
            full = full + between[i * BLOCK : (i + 1) * BLOCK, i * BLOCK : (i + 1) * BLOCK]
            trace += jnp.sum(jnp.where(rows == cols, full, 0.0), axis=0, keepdims=True)
            a[low:high, i * BLOCK : (i + 1) * BLOCK] = full[: high - low]
    for i, j in OFF_DIAGONAL:
        low, high = EDGES[i], EDGES[i + 1]
        a[low:high, j * BLOCK : (j + 1) * BLOCK] = (
            pack[places[i, j] : places[i, j] + high - low, :]
            + between[low:high, j * BLOCK : (j + 1) * BLOCK]
        )
    load = 0.01 * (jnp.sum(trace, axis=1, keepdims=True) / BANDS)
    for i in range(4):
        low, high = EDGES[i], EDGES[i + 1]
        full = a[low:high, i * BLOCK : (i + 1) * BLOCK]
        height = high - low
        a[low:high, i * BLOCK : (i + 1) * BLOCK] = full + jnp.where(
            (rows == cols)[:height], load, 0.0
        )
    w_ref[...] = jnp.zeros_like(w_ref)
    square = a[0:BLOCK, 0:BLOCK]
    for k in range(4):
        low, high = EDGES[k], EDGES[k + 1]
        groups = [square[8 * g : 8 * g + 8, :] for g in range((high - low) // 8)]
        m = jnp.concatenate(inverse_factor(groups, held), 0)[:, : high - low]
        parts = split3(m)
        if high < BANDS:
            end = EDGES[k + 2]
            factor = split3(product_parts(split3(a[high:end, low:high]), parts, 1, 1))
            update = product_parts(factor, factor, 1, 1)
            square = a[high:end, high : high + BLOCK]
            if end - high == BLOCK:
                square = square - update
            else:
                square = jnp.concatenate([square[:, : end - high] - update, square[:, end - high :]], 1)
        if k:
            w_ref[low:high, :low] = product_parts(parts, split3(w_ref[low:high, :low]), 1, 0)
        w_ref[low:high, low:high] = m
        if high < BANDS:
            row = split3(w_ref[low:high, :high])
            w_ref[high:end, :high] = w_ref[high:end, :high] - product_parts(factor, row, 1, 0)
            if end < BANDS:
                below = split3(product_parts(split3(a[end:, low:high]), parts, 1, 1))
                a[end:, high:end] = a[end:, high:end] - product_parts(below, factor, 1, 1)
                a[end:, end:BANDS] = a[end:, end:BANDS] - product_parts(below, below, 1, 1)
                w_ref[end:, :high] = w_ref[end:, :high] - product_parts(below, row, 1, 0)


def output_kernel(
    n_line, pixels, where_ref, own_ref, deep_ref, dev_ref, w_ref, offsets_ref, selects_ref, near1, near2, far_ref, *rest
):
    (out1_ref, out2_ref, out3_ref, approx_ref), (d, small) = rest[:4], rest[4:]
    tile, line, samp = where_ref[0], where_ref[1], where_ref[2]
    bit = samp % 2
    offset_ref, select_ref = offsets_ref.at[samp, line], selects_ref.at[bit]
    tiles = dev_ref.shape[0]
    which = lax.broadcasted_iota(jnp.int32, (tiles, COUNT), 0)
    near = 1 - 2 * bit
    gains = jnp.where(which == tile, offset_ref[4:5, :], 0.0)
    for k, step in enumerate((near, -near, 2 * near, -2 * near)):
        gains += jnp.where(which == tile + n_line * step, offset_ref[k : k + 1, :], 0.0)
    shift = product(dev_ref[:, 0:BANDS], gains, 0, 0)
    together = LANES // FAR
    lane = lax.broadcasted_iota(jnp.int32, (FAR_ROWS, LANES), 1)
    for k in range(together):
        moved = pltpu.roll(far_ref[0:FAR_ROWS, :], LANES - FAR - k * FAR, 1)
        small[pl.ds(k, FAR_ROWS, stride=together), :] = jnp.where(lane >= LANES - FAR, moved, 0.0)
    lane = lax.broadcasted_iota(jnp.int32, (BANDS, LANES), 1) % WIDE
    scale = float(pixels) ** 0.5

    def keep(at, value):
        for k, part in enumerate(split3(value * scale)):
            d[k, :, at : at + LANES] = part

    deep = split3(jnp.concatenate([near1[:, LANES:], near2[:, LANES:]], 1))
    select = select_ref[...].astype(jnp.bfloat16)
    near_deep = lax.dot_general(
        jnp.concatenate(deep, 1),
        jnp.concatenate([select] * 3, 0),
        (((1,), (0,)), ((), ())),
        preferred_element_type=jnp.float32,
    )
    bases = ((WIDE - 2) * (1 - bit), (WIDE - 2) * bit)
    for sb in range(3):
        at = sb * LANES
        value = own_ref[:, at : at + LANES] + shift[:, at : at + LANES]
        for base, ref in zip(bases, (near1, near2)):
            moved = pltpu.roll(ref[:, 0:LANES], (base - 2 * sb + LANES) % LANES, 1)
            value += jnp.where((lane >= base) & (lane < base + 2), moved, 0.0)
        keep(at, value)
    keep(
        LEVEL1,
        deep_ref[...] + shift[:, LEVEL1:] + near_deep + small[...],
    )
    for low, high in ((0, 2 * BLOCK), (2 * BLOCK, BANDS)):
        w = split3(w_ref[low:high, :high])
        out = product_parts(w, [d[k, 0:high, :] for k in range(3)], 1, 0)
        for sb in range(3):
            out1_ref[sb * BANDS + low : sb * BANDS + high, :] = out[:, sb * LANES : (sb + 1) * LANES]
        small[low:high, :] = out[:, LEVEL1:]
    size2, size3 = COUNT // 16, COUNT // 64
    rows2, rows3 = BANDS * size2 // LANES, BANDS * size3 // LANES
    for sb in range(3):
        out2_ref[sb * rows2 : (sb + 1) * rows2, :] = repacked(small, sb * size2, size2)
        out3_ref[sb * rows3 : (sb + 1) * rows3, :] = repacked(small, 3 * size2 + sb * size3, size3)
    approx_ref[...] = repacked(small, 3 * size2 + 3 * size3, size3)


def permuted(array, axis, partner):
    count = lax.axis_size(axis)
    return lax.ppermute(array, axis, [(i, partner(i)) for i in range(count) if 0 <= partner(i) < count])


def mirrored(size):
    def partner(i):
        within = i % size
        return i - within + 2 * (size // 2 - 1 - within // 2) + within % 2

    return partner


VMEM = pl.BlockSpec(memory_space=pltpu.VMEM)
SMEM = pl.BlockSpec(memory_space=pltpu.SMEM)


def call(kernel, name, shapes, inputs, scratch, flops):
    specs = [SMEM if value.dtype == jnp.int32 and value.ndim == 1 else VMEM for value in inputs]
    size = sum(value.size * 4 for value in inputs)
    return pl.pallas_call(
        kernel,
        name=name,
        out_shape=[
            shape if isinstance(shape, jax.ShapeDtypeStruct) else jax.ShapeDtypeStruct(shape, jnp.float32)
            for shape in shapes
        ],
        in_specs=specs,
        out_specs=[VMEM] * len(shapes),
        scratch_shapes=[pltpu.VMEM(shape, dtype) for shape, dtype in scratch],
        compiler_params=pltpu.CompilerParams(vmem_limit_bytes=16 * 2**20),
        cost_estimate=pl.CostEstimate(flops=flops, bytes_accessed=size, transcendentals=0),
    )(*inputs)


def local(constants, cube):
    line_table, samp_table, offset_table, select_table, relayed = (jnp.asarray(table) for table in constants)
    n_samp, n_line = lax.axis_size("samp"), lax.axis_size("line")
    tiles = n_samp * n_line
    samp, line = lax.axis_index("samp"), lax.axis_index("line")
    where = jnp.stack([samp * n_line + line, line, samp]).astype(jnp.int32)
    f32, bf16 = jnp.float32, jnp.bfloat16
    x = cube.reshape(BANDS * COUNT // LANES, LANES)
    other = permuted(x, "line", lambda i: i ^ 1)
    _, total = payload_rows(tiles)
    half, quarter = total // 2, total // 4
    lines, samps = line_table[line, samp & 1], samp_table[samp]
    send, keep, mean = call(
        functools.partial(gram_kernel, tiles),
        "gram",
        [(half, LANES), (half, LANES), (BANDS, LANES)],
        [where, x],
        [((3, 4 * BLOCK, COUNT), bf16), ((total, LANES), f32)],
        2 * BANDS * BANDS * COUNT * 4,
    )
    summed = keep + permuted(send, "line", lambda i: i ^ 1)
    side = ((samp >> 1) ^ (samp >> 2)) & 1
    kept = lax.dynamic_slice_in_dim(summed, side * quarter, quarter, 0)
    given = lax.dynamic_slice_in_dim(summed, (1 - side) * quarter, quarter, 0)

    mean, given, other, samps, lines = lax.optimization_barrier((mean, given, other, samps, lines))
    strip, near1, far = call(
        first_kernel,
        "first",
        [jax.ShapeDtypeStruct((3, BANDS, 2 * COUNT), bf16), (BANDS, 2 * LANES), (FAR_HELD, LANES)],
        [where, x, other, mean, lines, samps],
        [((3, 2 * COUNT, 2 * LANES), bf16), ((BANDS, LANES), f32)],
        2 * BANDS * 2 * COUNT * 3 * LANES * 6,
    )
    kept = kept + permuted(given, "samp", lambda i: i ^ 2)
    kept, near1, far, strip = lax.optimization_barrier((kept, near1, far, strip))
    near2, own_deep = call(
        second_kernel,
        "second",
        [(BANDS, 2 * LANES), (BANDS, LANES)],
        [strip, lines, samps],
        [((3, 2 * COUNT, 2 * LANES), bf16)],
        2 * BANDS * 2 * COUNT * 3 * LANES * 6,
    )
    kept = kept + permuted(kept, "samp", lambda i: i ^ 1)
    kept, near1, near2, own_deep, far, strip = lax.optimization_barrier(
        (kept, near1, near2, own_deep, far, strip)
    )
    near1 = permuted(near1, "samp", lambda i: i ^ 1)
    (own,) = call(
        third_kernel,
        "third",
        [(BANDS, LEVEL1)],
        [strip, lines, samps],
        [((3, SHALLOW, LEVEL1), bf16)],
        2 * BANDS * 2 * COUNT * 3 * LANES * 6,
    )
    size = 8
    while size <= n_samp:
        kept = kept + permuted(kept, "samp", mirrored(size))
        size *= 2
    kept, own, far = lax.optimization_barrier((kept, own, far))
    far = permuted(far, "samp", lambda i: min(i + 2, n_samp - 2 + (n_samp - 1 > i) * 1) if i & 1 else max(i - 2, int(i == 0)))
    back = permuted(kept, "samp", lambda i: i ^ 2)
    mine = jnp.where(side == 0, jnp.concatenate([kept, back]), jnp.concatenate([back, kept]))
    theirs = permuted(mine, "line", lambda i: i ^ 1)
    on = jnp.concatenate([jnp.zeros_like(relayed), relayed], 2)[1 - (samp & 1)]
    near2 = permuted(jnp.where(on, near1, near2), "samp", lambda i: min(max(((i + 1) ^ 1) - 1, 0), n_samp - 1))

    w, dev = call(
        functools.partial(whiten_kernel, tiles),
        "whiten",
        [(BANDS, BANDS), (tiles, 4 * BLOCK)],
        [where, mine, theirs],
        [((total, LANES), f32), ((BANDS, 4 * BLOCK), f32), ((2, 16, 8, LANES), f32)],
        10**8,
    )
    outs = call(
        functools.partial(output_kernel, n_line, COUNT * tiles),
        "outputs",
        [
            (3 * BANDS * (COUNT // 4) // LANES, LANES),
            (3 * BANDS * (COUNT // 16) // LANES, LANES),
            (3 * BANDS * (COUNT // 64) // LANES, LANES),
            (BANDS * (COUNT // 64) // LANES, LANES),
        ],
        [where, own, own_deep, dev, w, offset_table, select_table, near1, near2, far],
        [((3, BANDS, COUNT), bf16), ((BANDS, LANES), f32)],
        2 * BANDS * BANDS * COUNT * 6,
    )
    return tuple(out.reshape(-1) for out in outs)


def solution(mesh):
    n_samp, n_line = mesh.shape["samp"], mesh.shape["line"]
    assert n_line == 2 and n_samp >= 8 and n_samp & (n_samp - 1) == 0
    constants = build_constants(n_samp, n_line)
    spec = P(("groups", "samp", "line"))
    return jax.shard_map(
        functools.partial(local, constants),
        mesh=mesh,
        in_specs=(spec,),
        out_specs=(spec,) * 4,
        check_vma=False,
    )
```
